32 devices in a mesh: batch: 8 (over z, y), blk: 4 (over x, core).
Axes of the slice: x: 2, y: 2, z: 4, core: 2. Of those that a mesh axis runs over, the one named last changes fastest.
Arguments:
- tokens: bfloat16 [16, 1024, 768], P('batch', 'blk'), may hold values from -6 to 6
- segment_ids: int32 [16, 1024], P('batch', 'blk'), may hold values from 0 to 1023, as said below
- keep_flags: int32 [16], P('batch'), may hold values from 0 to 1, as said below
- input_weight: bfloat16 [768, 2304], replicated, may hold values from -0.21875 to 0.21875
- query_bias: bfloat16 [768], replicated, may hold values from -3 to 3
- value_bias: bfloat16 [768], replicated, may hold values from -3 to 3
- output_weight: bfloat16 [768, 768], replicated, may hold values from -0.875 to 0.875
- output_bias: bfloat16 [768], replicated, may hold values from -3 to 3
- first_gain: bfloat16 [768], replicated, may hold values from 0.099609375 to 1.8984375
- first_shift: bfloat16 [768], replicated, may hold values from -3 to 3
- up_weight: bfloat16 [768, 3072], replicated, may hold values from -0.21875 to 0.21875
- up_bias: bfloat16 [3072], replicated, may hold values from -3 to 3
- down_weight: bfloat16 [3072, 768], replicated, may hold values from -0.109375 to 0.109375
- down_bias: bfloat16 [768], replicated, may hold values from -3 to 3
- second_gain: bfloat16 [768], replicated, may hold values from 0.099609375 to 1.8984375
- second_shift: bfloat16 [768], replicated, may hold values from -3 to 3
- cotangent: bfloat16 [16, 1024, 768], P('batch', 'blk'), may hold values from -6 to 6
Outputs:
- mixed: bfloat16 [16, 1024, 768], P('batch', 'blk')
- tokens_grad: bfloat16 [16, 1024, 768], P('batch', 'blk')
- kept: int32 [], replicated
- input_weight_grad: float32 [768, 2304], replicated
- query_bias_grad: float32 [768], replicated
- value_bias_grad: float32 [768], replicated
- output_weight_grad: float32 [768, 768], replicated
- output_bias_grad: float32 [768], replicated
- first_gain_grad: float32 [768], replicated
- first_shift_grad: float32 [768], replicated
- up_weight_grad: float32 [768, 3072], replicated
- up_bias_grad: float32 [3072], replicated
- down_weight_grad: float32 [3072, 768], replicated
- down_bias_grad: float32 [768], replicated
- second_gain_grad: float32 [768], replicated
- second_shift_grad: float32 [768], replicated
The draws below stay inside these ranges and needn't reach their ends.
Inputs may be any that keep to these rules, and one draw needn't show every extreme that they name: `segment_ids`: every row begins with segment 0 and its ids never fall along the row, rising by at most one from token to token. `keep_flags`: among the 2 rows of each index of batch at least one is kept.
All inputs are finite; a program needn't handle non-finite values.
Results may differ from the reference program's by a relative error of at most 0.018.
Values may be sent and summed in bfloat16 or wider, within the bound.
A program may use at most 192 MiB of HBM per device.

```python
import jax
import jax.numpy as jnp
from jax import lax

HEADS = 12
HEAD_DIM = 64
D = 768
FF = 3072
ROWS_DEV = 2
BLOCK_TOK = 256
SEQ = 1024
ROWS = 16


def draw_segment_ids(key, part):
    key = jax.random.fold_in(key, 11)
    cut_key, pick_key = jax.random.split(key)
    groups = ROWS // ROWS_DEV
    mean_length = max(SEQ // 4, 2)
    rolls = jax.random.randint(cut_key, (ROWS, SEQ), 0, mean_length)
    cuts = (rolls == 0).astype(jnp.int32)
    position = jnp.arange(SEQ)[None, :]
    chosen = jax.random.randint(pick_key, (groups, 1), 0, ROWS_DEV)
    local_row = jnp.arange(ROWS_DEV)[None, :]
    long_row = (local_row == chosen).reshape(ROWS, 1)
    last_group = jnp.arange(groups)[:, None] == groups - 1
    single_row = (last_group & (local_row == (chosen + 1) % ROWS_DEV)).reshape(ROWS, 1)
    allowed = jnp.where(long_row, position < BLOCK_TOK, True) & (position > 0)
    cuts = jnp.where(allowed, cuts, 0)
    cuts = jnp.where(single_row & (position > 0), 1, cuts)
    return jnp.cumsum(cuts, axis=1).astype(jnp.int32)


def draw_keep_flags(key, part):
    key = jax.random.fold_in(key, 23)
    order_key, count_key = jax.random.split(key)
    groups = ROWS // ROWS_DEV
    order = jax.random.permutation(order_key, ROWS).reshape(groups, ROWS_DEV)
    rank = jnp.sum((order[:, None, :] < order[:, :, None]).astype(jnp.int32), axis=2)
    wobble = jax.random.randint(count_key, (groups,), -1, 2)
    wanted = 1 + 3 * jnp.arange(groups) // groups + wobble
    wanted = jnp.clip(wanted, 1, ROWS_DEV)
    return (rank < wanted[:, None]).astype(jnp.int32).reshape(ROWS)


def level_of(rng, shape, cuts, smallest, largest):
    def one(axis_at, blocks):
        steps = jax.random.uniform(jax.random.fold_in(jax.random.fold_in(rng, 6), axis_at), (blocks,), jnp.float32, smallest / len(cuts), largest / len(cuts))
        return jnp.repeat(jnp.exp(steps), shape[axis_at] // blocks).reshape((-1,) + (1,) * (len(shape) - axis_at - 1))

    level = one(*cuts[0])
    for cut in cuts[1:]:
        level = level * one(*cut)
    return level


def gaussian(rng, shape, deviation, limit, pieces=(), dtype=jnp.bfloat16):
    values = deviation * jax.random.normal(rng, shape, jnp.float32)
    if pieces:
        values = values * level_of(rng, shape, pieces, -0.22, 0.18)
    return jnp.clip(values, -limit, limit).astype(dtype)


def setup_inputs(seed: int = 0) -> dict:
    seeds = jax.random.split(jax.random.key(seed), 18)
    tokens = gaussian(seeds[0], (ROWS, SEQ, D), 1.0, 6.0, ((0, 8), (1, 4)))
    segment_ids = draw_segment_ids(jax.random.fold_in(seeds[17], 71), 0)
    keep_flags = draw_keep_flags(jax.random.fold_in(seeds[17], 71), 0)
    input_weight = gaussian(seeds[3], (D, 3 * D), D ** -0.5, 0.21875)
    query_bias = gaussian(seeds[4], (D,), 0.5, 3.0)
    value_bias = gaussian(seeds[5], (D,), 0.5, 3.0)
    output_weight = gaussian(seeds[6], (D, D), (D // 16) ** -0.5, 0.875)
    output_bias = gaussian(seeds[7], (D,), 0.5, 3.0)
    first_gain = jnp.clip(1.0 + 0.18 * jax.random.normal(seeds[8], (D,), jnp.float32), 0.099609375, 1.8984375).astype(jnp.bfloat16)
    first_shift = gaussian(seeds[9], (D,), 0.5, 3.0)
    up_weight = gaussian(seeds[10], (D, FF), D ** -0.5, 0.21875)
    up_bias = gaussian(seeds[11], (FF,), 0.5, 3.0)
    down_weight = gaussian(seeds[12], (FF, D), FF ** -0.5, 0.109375)
    down_bias = gaussian(seeds[13], (D,), 0.5, 3.0)
    second_gain = jnp.clip(1.0 + 0.18 * jax.random.normal(seeds[14], (D,), jnp.float32), 0.099609375, 1.8984375).astype(jnp.bfloat16)
    second_shift = gaussian(seeds[15], (D,), 0.5, 3.0)
    cotangent = gaussian(seeds[16], (ROWS, SEQ, D), 1.0, 6.0, ((0, 8), (1, 4)))
    return {"tokens": tokens, "segment_ids": segment_ids, "keep_flags": keep_flags, "input_weight": input_weight, "query_bias": query_bias, "value_bias": value_bias, "output_weight": output_weight, "output_bias": output_bias, "first_gain": first_gain, "first_shift": first_shift, "up_weight": up_weight, "up_bias": up_bias, "down_weight": down_weight, "down_bias": down_bias, "second_gain": second_gain, "second_shift": second_shift, "cotangent": cotangent}


@jax.custom_vjp
def low(v):
    return lax.optimization_barrier(v.astype(jnp.bfloat16)).astype(jnp.float32)

@jax.custom_vjp
def low_back(v):
    return v

def low_keep(v):
    return (low(v), None)

def low_pass(kept, grad):
    return (grad,)

def back_keep(v):
    return (v, None)

def back_low(kept, grad):
    return (low(grad),)
low.defvjp(low_keep, low_pass)
low_back.defvjp(back_keep, back_low)

def matmul(left, right):
    return jnp.dot(left, right, precision=lax.Precision.HIGHEST)

def layer_norm(values, gain, shift):
    center = lax.optimization_barrier(jnp.mean(values, axis=-1, keepdims=True))
    centered = values - center
    spread = lax.optimization_barrier(jnp.mean(centered * centered, axis=-1, keepdims=True))
    return centered * lax.rsqrt(spread + 1e-05) * gain + shift

@jax.checkpoint
def attend_row(parts):
    query, keys, values, segments = parts
    raw = jnp.einsum('qhd,khd->hqk', query, keys, precision=lax.Precision.HIGHEST) * HEAD_DIM ** (-0.5)
    raw = low_back(raw)
    same = segments[:, None] == segments[None, :]
    scores = jnp.where(same[None], raw, -1e+30)
    top = lax.optimization_barrier(jnp.max(scores, axis=-1, keepdims=True))
    powered = jnp.exp(scores - top)
    chance = low(powered / lax.optimization_barrier(jnp.sum(powered, axis=-1, keepdims=True)))
    return jnp.einsum('hqk,khd->qhd', chance, values, precision=lax.Precision.HIGHEST)

def forward(block_tokens, segments, row_scale, input_weight, query_bias, value_bias, output_weight, output_bias, first_gain, first_shift, up_weight, up_bias, down_weight, down_bias, second_gain, second_shift):
    group = block_tokens.shape[0]
    flat = block_tokens.reshape(group * SEQ, D)
    joined = matmul(flat, input_weight)
    query = low_back(low(joined[:, :D] + query_bias))
    keys = low_back(low(joined[:, D:2 * D]))
    values = low_back(low(joined[:, 2 * D:] + value_bias))
    shape = (group, SEQ, HEADS, HEAD_DIM)
    attended = lax.map(attend_row, (query.reshape(shape), keys.reshape(shape), values.reshape(shape), segments))
    attended = low_back(low(attended.reshape(group * SEQ, D)))
    branch = low_back(matmul(attended, output_weight) + output_bias)
    scale = jnp.repeat(row_scale, SEQ)[:, None]
    first = layer_norm(flat + scale * branch, first_gain, first_shift)
    hidden_pre = low_back(matmul(low(first), up_weight) + up_bias)
    hidden = low(jax.nn.gelu(hidden_pre, approximate=False))
    ffn = low_back(matmul(hidden, down_weight) + down_bias)
    return layer_norm(first + scale * ffn, second_gain, second_shift)

def reference(tokens, segment_ids, keep_flags, input_weight, query_bias, value_bias, output_weight, output_bias, first_gain, first_shift, up_weight, up_bias, down_weight, down_bias, second_gain, second_shift, cotangent):
    kept = jnp.sum(keep_flags).astype(jnp.int32)
    row_scale = keep_flags.astype(jnp.float32) * (ROWS / kept.astype(jnp.float32))
    weights = tuple((w.astype(jnp.float32) for w in (input_weight, query_bias, value_bias, output_weight, output_bias, first_gain, first_shift, up_weight, up_bias, down_weight, down_bias, second_gain, second_shift)))
    groups = ROWS // ROWS_DEV
    items = (tokens.reshape(groups, ROWS_DEV, SEQ, D), segment_ids.reshape(groups, ROWS_DEV, SEQ), row_scale.reshape(groups, ROWS_DEV), cotangent.reshape(groups, ROWS_DEV * SEQ, D))

    def group_step(totals, item):
        block_tokens, block_segments, block_scale, block_cot = item

        def run(inputs, *params):
            return forward(inputs, block_segments, block_scale, *params)
        result, pull = jax.vjp(run, block_tokens.astype(jnp.float32), *weights)
        grads = pull(block_cot.astype(jnp.float32))
        totals = tuple((a + b for a, b in zip(totals, grads[1:])))
        return (totals, (result.astype(jnp.bfloat16), grads[0].astype(jnp.bfloat16)))
    zeros = tuple((jnp.zeros_like(w) for w in weights))
    totals, outputs = lax.scan(group_step, zeros, items)
    mixed = outputs[0].reshape(ROWS, SEQ, D)
    tokens_grad = outputs[1].reshape(ROWS, SEQ, D)
    return (mixed, tokens_grad, kept, totals[0], totals[1], totals[2], totals[3], totals[4], totals[5], totals[6], totals[7], totals[8], totals[9], totals[10], totals[11], totals[12])
```

```python
from functools import partial

import jax
import jax.numpy as jnp
from jax import lax
from jax.experimental import pallas as pl
from jax.experimental.pallas import tpu as pltpu
from jax.sharding import PartitionSpec as P

HEAD_DIM = 64


masked_score = -1e30
norm_eps = 1e-05


MESH = pl.DeviceIdType.MESH
SPLIT = {"core": 2, "x": 2, "y": 2, "z": 4}
ORDERS = (("x", "y", "z"), ("y", "x", "z"), ("x", "z", "y"), ("y", "z", "x"))


def coordinates():
    batch, blk = lax.axis_index("batch"), lax.axis_index("blk")
    return {
        "core": lax.rem(blk, 2),
        "x": lax.div(blk, 2),
        "y": lax.rem(batch, 2),
        "z": lax.rem(lax.div(batch, 2), 4),
        "far": lax.div(batch, 8),
    }


def device_at(place, **changes):
    at = {**place, **changes}
    return (at["far"] * 8 + at["z"] * 2 + at["y"], at["x"] * 2 + at["core"])


def flipped(index, bit):
    return index + bit - 2 * bit * lax.rem(lax.div(index, bit), 2)


def far_bits(far):
    return [1 << b for b in range(far.bit_length() - 1)]


def greet(place, far):
    partners = [device_at(place, **{d: 1 - place[d]}) for d in ("core", "x", "y")]
    partners += [device_at(place, z=lax.rem(place["z"] + s, 4)) for s in (1, 2, 3)]
    partners += [device_at(place, far=flipped(place["far"], bit)) for bit in far_bits(far)]
    barrier = pltpu.get_barrier_semaphore()
    for partner in partners:
        pl.semaphore_signal(barrier, inc=1, device_id=partner, device_id_type=MESH)
    pl.semaphore_wait(barrier, len(partners))


class Chunk:
    def __init__(self, matrix, row, row_step, col, col_step, width, order, far):
        self.matrix, self.width, self.order, self.far = matrix, width, order, far
        self.row, self.row_step, self.col, self.col_step = row, row_step, col, col_step
        self.received = 768
        self.copies = 2
        rows = 768
        for d in order:
            rows //= SPLIT[d]
            self.received += (SPLIT[d] - 1) * rows
            self.copies += 2 * (SPLIT[d] - 1)
        self.share = rows
        self.received += rows * len(far_bits(far))
        self.copies += len(far_bits(far))

    def region(self, ref, half, row, rows):
        row = self.row + half * self.row_step + row
        col = self.col + half * self.col_step
        return ref.at[
            pl.ds(pl.multiple_of(row, 16), rows), pl.ds(pl.multiple_of(col, 128), self.width)
        ]

    def steps(self, place, own, whole, inbox, send_sems, recv_sems, store_sem):
        sent = []

        def send(source, target, device):
            i = len(sent)
            copy = pltpu.make_async_remote_copy(
                src_ref=source,
                dst_ref=target,
                send_sem=send_sems.at[i],
                recv_sem=recv_sems.at[i],
                device_id=device,
                device_id_type=MESH,
            )
            copy.start()
            sent.append(copy)
            return copy

        def add(row, rows, froms):
            tile = min(rows, 48)

            def one(t, carry):
                at = pl.multiple_of(t * tile, 16)
                here = self.region(own, core, row + at, tile)
                total = here[...].astype(jnp.float32)
                for start in froms:
                    total = total + inbox[pl.ds(pl.multiple_of(start + at, 16), tile), :].astype(
                        jnp.float32
                    )
                here[...] = total.astype(jnp.bfloat16)
                return carry

            lax.fori_loop(0, rows // tile, one, 0)

        core = place["core"]
        copy = send(
            self.region(own, 1 - core, 0, 768),
            inbox.at[pl.ds(0, 768)],
            device_at(place, core=1 - core),
        )
        yield
        copy.wait_recv()
        add(0, 768, (0,))
        row, rows, used = 0, 768, 768
        for d in self.order:
            parts, index = SPLIT[d], place[d]
            rows //= parts
            copies = []
            for s in range(parts - 1):
                other = lax.rem(index + 1 + s, parts)
                copies.append(
                    send(
                        self.region(own, core, row + other * rows, rows),
                        inbox.at[pl.ds(used + s * rows, rows)],
                        device_at(place, **{d: other}),
                    )
                )
            row = row + index * rows
            yield
            for copy in copies:
                copy.wait_recv()
            add(row, rows, [used + s * rows for s in range(parts - 1)])
            used += (parts - 1) * rows
        for bit in far_bits(self.far):
            copy = send(
                self.region(own, core, row, rows),
                inbox.at[pl.ds(used, rows)],
                device_at(place, far=flipped(place["far"], bit)),
            )
            yield
            copy.wait_recv()
            copy.wait_send()
            sent[-1] = None
            add(row, rows, (used,))
            used += rows
        store = pltpu.make_async_copy(
            self.region(own, core, row, rows), self.region(whole, core, row, rows), store_sem
        )
        store.start()
        source = own
        for d in reversed(self.order):
            parts, index = SPLIT[d], place[d]
            copies = []
            for s in range(parts - 1):
                other = lax.rem(index + 1 + s, parts)
                copies.append(
                    send(
                        self.region(source, core, row, rows),
                        self.region(whole, core, row, rows),
                        device_at(place, **{d: other}),
                    )
                )
            yield
            for copy in copies:
                copy.wait_recv()
            if source is own:
                store.wait()
            source = whole
            row = row - index * rows
            rows *= parts
        copy = send(
            self.region(whole, core, 0, 768),
            self.region(whole, core, 0, 768),
            device_at(place, core=1 - core),
        )
        yield
        copy.wait_recv()
        for copy in sent:
            if copy is not None:
                copy.wait_send()


def vector_hops(place, far):
    hops = [device_at(place, **{d: 1 - place[d]}) for d in ("core", "x", "y")]
    hops += [device_at(place, z=flipped(place["z"], bit)) for bit in (1, 2)]
    hops += [device_at(place, far=flipped(place["far"], bit)) for bit in far_bits(far)]
    return hops


def vector_steps(place, far, vectors, totals, inbox, send_sems, recv_sems):
    held, sent = vectors, []
    for i, device in enumerate(vector_hops(place, far)):
        copy = pltpu.make_async_remote_copy(
            src_ref=held,
            dst_ref=inbox.at[i],
            send_sem=send_sems.at[i],
            recv_sem=recv_sems.at[i],
            device_id=device,
            device_id_type=MESH,
        )
        copy.start()
        sent.append(copy)
        yield
        copy.wait_recv()
        totals.at[i][...] = held[...] + inbox[i]
        held = totals.at[i]
    for copy in sent:
        copy.wait_send()


def chunks_of(far):
    x, y, xz, yz = ORDERS
    return (
        Chunk("down", 0, 768, 0, 0, 768, x, far),
        Chunk("down", 1536, 768, 0, 0, 768, y, far),
        Chunk("up", 0, 0, 0, 768, 768, xz, far),
        Chunk("up", 0, 0, 1536, 768, 768, yz, far),
        Chunk("out", 0, 0, 0, 384, 384, x, far),
        Chunk("in", 0, 0, 0, 384, 384, y, far),
        Chunk("in", 0, 0, 768, 384, 384, x, far),
        Chunk("in", 0, 0, 1536, 384, 384, y, far),
    )


def run_in_turn(steps):
    steps = list(steps)
    while steps:
        left = []
        for step in steps:
            try:
                next(step)
                left.append(step)
            except StopIteration:
                pass
        steps = left


MATRICES = (("in", 768, 2304), ("out", 768, 768), ("up", 768, 3072), ("down", 3072, 768))


def sum_kernel(far, *refs):
    names = [m[0] for m in MATRICES]
    given = dict(zip(names, refs[:4]))
    vectors = refs[4]
    whole = dict(zip(names, refs[5:9]))
    vector_out = refs[9]
    own = dict(zip(names, refs[10:14]))
    chunks = chunks_of(far)
    n = len(chunks)
    inboxes = refs[14 : 14 + n]
    vec_inbox, vec_totals, send_sems, recv_sems, vec_send, vec_recv, load_sems, store_sems = refs[14 + n :]
    place = coordinates()
    loads = []
    for i, chunk in enumerate(chunks):
        rows = 768 + chunk.row_step
        cols = chunk.width + chunk.col_step
        part = (pl.ds(chunk.row, rows), pl.ds(chunk.col, cols))
        load = pltpu.make_async_copy(
            given[chunk.matrix].at[part], own[chunk.matrix].at[part], load_sems.at[i]
        )
        load.start()
        loads.append(load)
    greet(place, far)
    gens = []
    used = 0
    for i, chunk in enumerate(chunks):
        loads[i].wait()
        span = pl.ds(used, chunk.copies)
        used += chunk.copies
        gens.append(
            chunk.steps(
                place,
                own[chunk.matrix],
                whole[chunk.matrix],
                inboxes[i],
                send_sems.at[span],
                recv_sems.at[span],
                store_sems.at[i],
            )
        )
        next(gens[-1])
    gens.append(vector_steps(place, far, vectors, vec_totals, vec_inbox, vec_send, vec_recv))
    run_in_turn(gens)
    vector_out[...] = vec_totals[len(vector_hops(place, far)) - 1]


def summed_gradients(grads, vectors, far):
    chunks = chunks_of(far)
    hops = 5 + len(far_bits(far))
    copies = sum(c.copies for c in chunks)
    rows, width = vectors.shape
    return pl.pallas_call(
        partial(sum_kernel, far),
        out_shape=[jax.ShapeDtypeStruct((a, b), jnp.bfloat16) for _, a, b in MATRICES]
        + [jax.ShapeDtypeStruct(vectors.shape, jnp.float32)],
        in_specs=[pl.BlockSpec(memory_space=pl.ANY)] * 4 + [pl.BlockSpec(memory_space=pltpu.VMEM)],
        out_specs=[pl.BlockSpec(memory_space=pl.ANY)] * 4 + [pl.BlockSpec(memory_space=pltpu.VMEM)],
        scratch_shapes=[pltpu.VMEM((a, b), jnp.bfloat16) for _, a, b in MATRICES]
        + [pltpu.VMEM((c.received, c.width), jnp.bfloat16) for c in chunks]
        + [
            pltpu.VMEM((hops, rows, width), jnp.float32),
            pltpu.VMEM((hops, rows, width), jnp.float32),
            pltpu.SemaphoreType.DMA((copies,)),
            pltpu.SemaphoreType.DMA((copies,)),
            pltpu.SemaphoreType.DMA((hops,)),
            pltpu.SemaphoreType.DMA((hops,)),
            pltpu.SemaphoreType.DMA((len(chunks),)),
            pltpu.SemaphoreType.DMA((len(chunks),)),
        ],
        compiler_params=pltpu.CompilerParams(
            collective_id=0, has_side_effects=True, vmem_limit_bytes=56 << 20
        ),
        name="gradient_sum",
    )(*grads, vectors)


def passed_along(block, axis, distance):
    devices = range(lax.axis_size(axis))
    route = [((i - distance) % len(devices), i) for i in devices]
    return lax.ppermute(block, axis, route)


def norm_forward(values, gain, shift):
    center = jnp.mean(values, axis=-1, keepdims=True)
    centered = values - center
    spread = jnp.mean(centered * centered, axis=-1, keepdims=True)
    inverse = lax.rsqrt(spread + norm_eps)
    normed = centered * inverse
    return (normed * gain + shift, normed, inverse)


def norm_backward(grad_out, normed, inverse, gain):
    gain_grad = jnp.sum(grad_out * normed, axis=0)
    shift_grad = jnp.sum(grad_out, axis=0)
    scaled = grad_out * gain
    inner = (
        scaled
        - jnp.mean(scaled, axis=-1, keepdims=True)
        - normed * jnp.mean(scaled * normed, axis=-1, keepdims=True)
    )
    return (inverse * inner, gain_grad, shift_grad)


def block_scores(query, key_block, query_segments, key_segments):
    raw = jnp.einsum(
        "rqhd,rkhd->rhqk", query, key_block, preferred_element_type=jnp.float32
    ) * HEAD_DIM ** (-0.5)
    same = query_segments[:, None, :, None] == key_segments[:, None, None, :]
    return jnp.where(same, raw, masked_score)


def body(
    tokens,
    segment_ids,
    keep_flags,
    input_weight,
    query_bias,
    value_bias,
    output_weight,
    output_bias,
    first_gain,
    first_shift,
    up_weight,
    up_bias,
    down_weight,
    down_bias,
    second_gain,
    second_shift,
    cotangent,
):
    rows, cols, width = tokens.shape
    heads = width // HEAD_DIM
    cycle = lax.axis_size("blk")
    place = lax.axis_index("blk")
    score_scale = HEAD_DIM ** (-0.5)
    kept_total = lax.psum(jnp.sum(keep_flags).astype(jnp.float32), "batch")
    rows_all = rows * lax.axis_size("batch")
    row_scale = keep_flags.astype(jnp.float32) * (rows_all / kept_total)
    token_scale = jnp.repeat(row_scale, cols)[:, None]
    whole_segments = lax.all_gather(segment_ids, "blk", axis=1, tiled=True)
    flat = tokens.reshape(rows * cols, width)
    joined = jnp.dot(flat, input_weight, preferred_element_type=jnp.float32)
    head_shape = (rows, cols, heads, HEAD_DIM)
    query = (
        (joined[:, :width] + query_bias.astype(jnp.float32))
        .astype(jnp.bfloat16)
        .reshape(head_shape)
    )
    keys = joined[:, width : 2 * width].astype(jnp.bfloat16).reshape(head_shape)
    values = (
        (joined[:, 2 * width :] + value_bias.astype(jnp.float32))
        .astype(jnp.bfloat16)
        .reshape(head_shape)
    )
    blocks = []
    carried_pair = (keys, values)
    for step in range(cycle):
        if step > 0:
            carried_pair = passed_along((carried_pair[0], carried_pair[1]), "blk", 1)
        blocks.append((carried_pair[0], carried_pair[1], (place - step) % cycle))
    run_max = jnp.full((rows, heads, cols), masked_score, jnp.float32)
    run_sum = jnp.zeros((rows, heads, cols), jnp.float32)
    kept_scores = []
    for key_block, value_block, owner in blocks:
        key_segments = lax.dynamic_slice_in_dim(whole_segments, owner * cols, cols, 1)
        scores = block_scores(query, key_block, segment_ids, key_segments)
        kept_scores.append(scores)
        new_max = jnp.maximum(run_max, jnp.max(scores, axis=-1))
        run_sum = run_sum * jnp.exp(run_max - new_max) + jnp.sum(
            jnp.exp(scores - new_max[..., None]), axis=-1
        )
        run_max = new_max
    log_total = run_max + jnp.log(run_sum)
    attended = jnp.zeros(head_shape, jnp.float32)
    for scores, (key_block, value_block, owner) in zip(kept_scores, blocks):
        chance = jnp.exp(scores - log_total[..., None]).astype(jnp.bfloat16)
        attended = attended + jnp.einsum(
            "rhqk,rkhd->rqhd", chance, value_block, preferred_element_type=jnp.float32
        )
    attended_low = attended.reshape(rows * cols, width).astype(jnp.bfloat16)
    branch = jnp.dot(
        attended_low, output_weight, preferred_element_type=jnp.float32
    ) + output_bias.astype(jnp.float32)
    first_gain_f = first_gain.astype(jnp.float32)
    second_gain_f = second_gain.astype(jnp.float32)
    first, normed_first, inverse_first = norm_forward(
        flat.astype(jnp.float32) + token_scale * branch,
        first_gain_f,
        first_shift.astype(jnp.float32),
    )
    first_low = first.astype(jnp.bfloat16)
    hidden_pre = jnp.dot(first_low, up_weight, preferred_element_type=jnp.float32) + up_bias.astype(
        jnp.float32
    )
    hidden_act, gelu_pull = jax.vjp(partial(jax.nn.gelu, approximate=False), hidden_pre)
    hidden = hidden_act.astype(jnp.bfloat16)
    ffn = jnp.dot(hidden, down_weight, preferred_element_type=jnp.float32) + down_bias.astype(
        jnp.float32
    )
    result, normed_second, inverse_second = norm_forward(
        first + token_scale * ffn, second_gain_f, second_shift.astype(jnp.float32)
    )
    mixed = result.astype(jnp.bfloat16).reshape(rows, cols, width)
    grad_out = cotangent.reshape(rows * cols, width).astype(jnp.float32)
    second_in_grad, second_gain_grad, second_shift_grad = norm_backward(
        grad_out, normed_second, inverse_second, second_gain_f
    )
    ffn_grad = (token_scale * second_in_grad).astype(jnp.bfloat16)
    down_weight_grad = jnp.einsum("tf,td->fd", hidden, ffn_grad, preferred_element_type=jnp.float32)
    down_bias_grad = jnp.sum(ffn_grad.astype(jnp.float32), axis=0)
    hidden_grad = jnp.einsum("td,fd->tf", ffn_grad, down_weight, preferred_element_type=jnp.float32)
    pre_grad = gelu_pull(hidden_grad)[0].astype(jnp.bfloat16)
    up_weight_grad = jnp.einsum(
        "td,tf->df", first_low, pre_grad, preferred_element_type=jnp.float32
    )
    up_bias_grad = jnp.sum(pre_grad.astype(jnp.float32), axis=0)
    first_out_grad = second_in_grad + jnp.einsum(
        "tf,df->td", pre_grad, up_weight, preferred_element_type=jnp.float32
    )
    first_in_grad, first_gain_grad, first_shift_grad = norm_backward(
        first_out_grad, normed_first, inverse_first, first_gain_f
    )
    branch_grad = (token_scale * first_in_grad).astype(jnp.bfloat16)
    output_weight_grad = jnp.einsum(
        "ta,tb->ab", attended_low, branch_grad, preferred_element_type=jnp.float32
    )
    output_bias_grad = jnp.sum(branch_grad.astype(jnp.float32), axis=0)
    attended_grad = (
        jnp.einsum("tb,ab->ta", branch_grad, output_weight, preferred_element_type=jnp.float32)
        .astype(jnp.bfloat16)
        .reshape(head_shape)
    )
    delta = jnp.einsum("rqhd,rqhd->rhq", attended_grad.astype(jnp.float32), attended)
    query_total = jnp.zeros(head_shape, jnp.float32)
    carried_grads = (jnp.zeros(head_shape, jnp.float32), jnp.zeros(head_shape, jnp.float32))
    for step in range(cycle):
        if step > 0:
            carried_grads = (
                passed_along(carried_grads[0].astype(jnp.bfloat16), "blk", -1).astype(jnp.float32),
                passed_along(carried_grads[1].astype(jnp.bfloat16), "blk", -1).astype(jnp.float32),
            )
        key_block, value_block, owner = blocks[cycle - 1 - step]
        contribution_key_segments = lax.dynamic_slice_in_dim(whole_segments, owner * cols, cols, 1)
        contribution_scores = block_scores(query, key_block, segment_ids, contribution_key_segments)
        contribution_chance = jnp.exp(contribution_scores - log_total[..., None])
        values_part = jnp.einsum(
            "rhqk,rqhd->rkhd",
            contribution_chance.astype(jnp.bfloat16),
            attended_grad,
            preferred_element_type=jnp.float32,
        )
        chance_grad = jnp.einsum(
            "rqhd,rkhd->rhqk", attended_grad, value_block, preferred_element_type=jnp.float32
        )
        score_grad = (contribution_chance * (chance_grad - delta[..., None])).astype(jnp.bfloat16)
        query_part = (
            jnp.einsum("rhqk,rkhd->rqhd", score_grad, key_block, preferred_element_type=jnp.float32)
            * score_scale
        )
        keys_part = (
            jnp.einsum("rhqk,rqhd->rkhd", score_grad, query, preferred_element_type=jnp.float32)
            * score_scale
        )
        query_part, keys_part, values_part = (query_part, keys_part, values_part)
        query_total = query_total + query_part
        carried_grads = (carried_grads[0] + keys_part, carried_grads[1] + values_part)
    keys_total, values_total = carried_grads
    flat_shape = (rows * cols, width)
    query_grad = query_total.astype(jnp.bfloat16).reshape(flat_shape)
    keys_grad = keys_total.astype(jnp.bfloat16).reshape(flat_shape)
    values_grad = values_total.astype(jnp.bfloat16).reshape(flat_shape)
    joined_grad = jnp.concatenate([query_grad, keys_grad, values_grad], axis=1)
    input_weight_grad = jnp.einsum(
        "td,te->de", flat, joined_grad, preferred_element_type=jnp.float32
    )
    query_bias_grad = jnp.sum(query_grad.astype(jnp.float32), axis=0)
    value_bias_grad = jnp.sum(values_grad.astype(jnp.float32), axis=0)
    tokens_grad = (
        (
            first_in_grad
            + jnp.einsum("te,de->td", joined_grad, input_weight, preferred_element_type=jnp.float32)
        )
        .astype(jnp.bfloat16)
        .reshape(rows, cols, width)
    )
    low = [g.astype(jnp.bfloat16) for g in (input_weight_grad, output_weight_grad, up_weight_grad, down_weight_grad)]
    vectors = jnp.stack(
        [
            query_bias_grad,
            value_bias_grad,
            output_bias_grad,
            first_gain_grad,
            first_shift_grad,
            down_bias_grad,
            second_gain_grad,
            second_shift_grad,
        ]
    )
    vectors = jnp.concatenate(
        [vectors, up_bias_grad.reshape(-1, width), jnp.zeros((4, width), jnp.float32)]
    )
    *low, vectors = summed_gradients(low, vectors, lax.axis_size("batch") // 8)
    full = [g.astype(jnp.float32) for g in low]
    return (
        mixed,
        tokens_grad,
        kept_total.astype(jnp.int32),
        full[0],
        vectors[0],
        vectors[1],
        full[1],
        vectors[2],
        vectors[3],
        vectors[4],
        full[2],
        vectors[8:12].reshape(-1),
        full[3],
        vectors[5],
        vectors[6],
        vectors[7],
    )


def solution(mesh):
    in_specs = (
        P("batch", "blk", None),
        P("batch", "blk"),
        P("batch"),
        P(),
        P(),
        P(),
        P(),
        P(),
        P(),
        P(),
        P(),
        P(),
        P(),
        P(),
        P(),
        P(),
        P("batch", "blk", None),
    )
    out_specs = (
        P("batch", "blk", None),
        P("batch", "blk", None),
        P(),
        P(),
        P(),
        P(),
        P(),
        P(),
        P(),
        P(),
        P(),
        P(),
        P(),
        P(),
        P(),
        P(),
    )
    return jax.shard_map(body, mesh=mesh, in_specs=in_specs, out_specs=out_specs, check_vma=False)
```

```python
from functools import partial

import jax
import jax.numpy as jnp
from jax import lax
from jax.experimental import pallas as pl
from jax.experimental.pallas import tpu as pltpu
from jax.sharding import PartitionSpec as P

HEAD_DIM = 64


masked_score = -1e30
norm_eps = 1e-05


MESH = pl.DeviceIdType.MESH
SPLIT = {"core": 2, "x": 2, "y": 2, "z": 4}
ORDERS = (("x", "y", "z"), ("y", "x", "z"), ("x", "z", "y"), ("y", "z", "x"))


def coordinates():
    batch, blk = lax.axis_index("batch"), lax.axis_index("blk")
    return {
        "core": lax.rem(blk, 2),
        "x": lax.div(blk, 2),
        "y": lax.rem(batch, 2),
        "z": lax.rem(lax.div(batch, 2), 4),
        "far": lax.div(batch, 8),
    }


def device_at(place, **changes):
    at = {**place, **changes}
    return (at["far"] * 8 + at["z"] * 2 + at["y"], at["x"] * 2 + at["core"])


def flipped(index, bit):
    return index + bit - 2 * bit * lax.rem(lax.div(index, bit), 2)


def far_bits(far):
    return [1 << b for b in range(far.bit_length() - 1)]


def greet(place, far, diagonal=False):
    partners = [device_at(place, **{d: 1 - place[d]}) for d in ("core", "x", "y")]
    partners += [device_at(place, z=lax.rem(place["z"] + s, 4)) for s in (1, 2, 3)]
    partners += [device_at(place, far=flipped(place["far"], bit)) for bit in far_bits(far)]
    if diagonal:
        partners.append(device_at(place, x=1 - place["x"], core=1 - place["core"]))
    barrier = pltpu.get_barrier_semaphore()
    for partner in partners:
        pl.semaphore_signal(barrier, inc=1, device_id=partner, device_id_type=MESH)
    pl.semaphore_wait(barrier, len(partners))


class Chunk:
    def __init__(self, matrix, row, row_step, col, col_step, width, order, far):
        self.matrix, self.width, self.order, self.far = matrix, width, order, far
        self.row, self.row_step, self.col, self.col_step = row, row_step, col, col_step
        self.received = 768
        self.copies = 2
        rows = 768
        for d in order:
            rows //= SPLIT[d]
            self.received += (SPLIT[d] - 1) * rows
            self.copies += 2 * (SPLIT[d] - 1)
        self.share = rows
        self.received += rows * len(far_bits(far))
        self.copies += len(far_bits(far))

    def region(self, ref, half, row, rows):
        row = self.row + half * self.row_step + row
        col = self.col + half * self.col_step
        return ref.at[
            pl.ds(pl.multiple_of(row, 16), rows), pl.ds(pl.multiple_of(col, 128), self.width)
        ]

    def steps(self, place, own, whole, inbox, send_sems, recv_sems, store_sem):
        sent = []

        def send(source, target, device):
            i = len(sent)
            copy = pltpu.make_async_remote_copy(
                src_ref=source,
                dst_ref=target,
                send_sem=send_sems.at[i],
                recv_sem=recv_sems.at[i],
                device_id=device,
                device_id_type=MESH,
            )
            copy.start()
            sent.append(copy)
            return copy

        def add(row, rows, froms):
            tile = min(rows, 48)

            def one(t, carry):
                at = pl.multiple_of(t * tile, 16)
                here = self.region(own, core, row + at, tile)
                total = here[...].astype(jnp.float32)
                for start in froms:
                    total = total + inbox[pl.ds(pl.multiple_of(start + at, 16), tile), :].astype(
                        jnp.float32
                    )
                here[...] = total.astype(jnp.bfloat16)
                return carry

            lax.fori_loop(0, rows // tile, one, 0)

        core = place["core"]
        copy = send(
            self.region(own, 1 - core, 0, 768),
            inbox.at[pl.ds(0, 768)],
            device_at(place, core=1 - core),
        )
        yield
        copy.wait_recv()
        add(0, 768, (0,))
        row, rows, used = 0, 768, 768
        for d in self.order:
            parts, index = SPLIT[d], place[d]
            rows //= parts
            copies = []
            for s in range(parts - 1):
                other = lax.rem(index + 1 + s, parts)
                copies.append(
                    send(
                        self.region(own, core, row + other * rows, rows),
                        inbox.at[pl.ds(used + s * rows, rows)],
                        device_at(place, **{d: other}),
                    )
                )
            row = row + index * rows
            yield
            for copy in copies:
                copy.wait_recv()
            add(row, rows, [used + s * rows for s in range(parts - 1)])
            used += (parts - 1) * rows
        for bit in far_bits(self.far):
            copy = send(
                self.region(own, core, row, rows),
                inbox.at[pl.ds(used, rows)],
                device_at(place, far=flipped(place["far"], bit)),
            )
            yield
            copy.wait_recv()
            copy.wait_send()
            sent[-1] = None
            add(row, rows, (used,))
            used += rows
        store = pltpu.make_async_copy(
            self.region(own, core, row, rows), self.region(whole, core, row, rows), store_sem
        )
        store.start()
        source = own
        for d in reversed(self.order):
            parts, index = SPLIT[d], place[d]
            copies = []
            for s in range(parts - 1):
                other = lax.rem(index + 1 + s, parts)
                copies.append(
                    send(
                        self.region(source, core, row, rows),
                        self.region(whole, core, row, rows),
                        device_at(place, **{d: other}),
                    )
                )
            yield
            for copy in copies:
                copy.wait_recv()
            if source is own:
                store.wait()
            source = whole
            row = row - index * rows
            rows *= parts
        copy = send(
            self.region(whole, core, 0, 768),
            self.region(whole, core, 0, 768),
            device_at(place, core=1 - core),
        )
        yield
        copy.wait_recv()
        for copy in sent:
            if copy is not None:
                copy.wait_send()


def vector_hops(place, far):
    hops = [device_at(place, **{d: 1 - place[d]}) for d in ("core", "x", "y")]
    hops += [device_at(place, z=flipped(place["z"], bit)) for bit in (1, 2)]
    hops += [device_at(place, far=flipped(place["far"], bit)) for bit in far_bits(far)]
    return hops


def vector_steps(place, far, totals, inbox, send_sems, recv_sems):
    sent = []
    for i, device in enumerate(vector_hops(place, far)):
        copy = pltpu.make_async_remote_copy(
            src_ref=totals.at[i],
            dst_ref=inbox.at[i],
            send_sem=send_sems.at[i],
            recv_sem=recv_sems.at[i],
            device_id=device,
            device_id_type=MESH,
        )
        copy.start()
        sent.append(copy)
        yield
        copy.wait_recv()
        totals[i + 1] = totals[i] + inbox[i]
    for copy in sent:
        copy.wait_send()


def chunks_of(far):
    x, y, xz, yz = ORDERS
    return (
        Chunk("down", 0, 768, 0, 0, 768, x, far),
        Chunk("down", 1536, 768, 0, 0, 768, y, far),
        Chunk("up", 0, 0, 0, 768, 768, xz, far),
        Chunk("up", 0, 0, 1536, 768, 768, yz, far),
        Chunk("out", 0, 0, 0, 384, 384, x, far),
        Chunk("in", 0, 0, 0, 384, 384, y, far),
        Chunk("in", 0, 0, 768, 384, 384, x, far),
        Chunk("in", 0, 0, 1536, 384, 384, y, far),
    )


def run_in_turn(steps):
    steps = list(steps)
    while steps:
        left = []
        for step in steps:
            try:
                next(step)
                left.append(step)
            except StopIteration:
                pass
        steps = left


MATRICES = (("in", 768, 2304), ("out", 768, 768), ("up", 768, 3072), ("down", 3072, 768))
F32, LOW = jnp.float32, jnp.bfloat16
PAIR = 2 * HEAD_DIM
VMEM_LIMIT = 60 << 20


def dot(left, right):
    return lax.dot_general(left, right, (((1,), (0,)), ((), ())), preferred_element_type=F32)


def dot_nt(left, right):
    return lax.dot_general(left, right, (((1,), (1,)), ((), ())), preferred_element_type=F32)


def span(start, size, unit):
    return pl.ds(pl.multiple_of(start, unit), size)


def lanes_of(i, rows):
    lane = lax.broadcasted_iota(jnp.int32, (rows, PAIR), 1)
    return lax.div(lane, HEAD_DIM) == i


def remote(source, target, send_sem, recv_sem, device):
    return pltpu.make_async_remote_copy(
        src_ref=source,
        dst_ref=target,
        send_sem=send_sem,
        recv_sem=recv_sem,
        device_id=device,
        device_id_type=MESH,
    )


def front_kernel(
    far,
    tokens,
    cot,
    segments,
    keep,
    weight,
    query_bias,
    value_bias,
    row_tokens,
    row_cot,
    query,
    keys,
    values,
    attended,
    log_total,
    bias,
    scale,
    kept,
    ids_out,
    ids_in,
    counts,
    count_in,
    values_t,
    send_sems,
    recv_sems,
    count_send,
    count_recv,
    local_sem,
):
    place = coordinates()
    x, core = place["x"], place["core"]
    cols = tokens.shape[1]
    half = 2 * cols
    width = tokens.shape[2]
    greet(place, far, diagonal=True)
    other_x = device_at(place, x=1 - x)
    other_core = device_at(place, core=1 - core)
    here, there = span(x * cols, cols, 256), span((1 - x) * cols, cols, 256)
    move_tokens = remote(
        tokens.at[1 - x], row_tokens.at[here], send_sems.at[0], recv_sems.at[0], other_x
    )
    move_tokens.start()
    for r in range(2):
        ids_out[r] = jnp.broadcast_to(segments[r : r + 1, :], (8, cols))
    blk = x * 2 + core
    moves = []
    for i, (dx, dc) in enumerate(((0, 1), (1, 0), (1, 1))):
        to_x = x + dx - 2 * dx * x
        to_core = core + dc - 2 * dc * core
        moves.append(
            remote(
                ids_out.at[to_x],
                ids_in.at[blk],
                send_sems.at[2 + i],
                recv_sems.at[2 + i],
                device_at(place, x=to_x, core=to_core),
            )
        )
        moves[-1].start()
    ids_in[blk] = ids_out[x]
    counts[0] = jnp.full((8, 128), (keep[0] + keep[1]).astype(F32), F32)
    hops = count_hops(place, far)
    count_moves = []

    def hop(i):
        if i:
            count_moves[-1].wait_recv()
            counts[i] = counts[i - 1] + count_in[i - 1]
        if i < len(hops):
            move = remote(
                counts.at[i], count_in.at[i], count_send.at[i], count_recv.at[i], hops[i]
            )
            move.start()
            count_moves.append(move)

    hop(0)
    move_cot = remote(cot.at[1 - x], row_cot.at[here], send_sems.at[1], recv_sems.at[1], other_x)
    move_cot.start()
    stay_cot = pltpu.make_async_copy(cot.at[x], row_cot.at[here_of(x, cols)], local_sem)
    stay_cot.start()
    row_tokens[here, :] = tokens[x]

    def project(rows, at):
        block = row_tokens[rows, :]
        query[rows, :] = (
            (dot(block, weight[:, :width]) + query_bias[...].astype(F32).reshape(1, -1)).astype(LOW)
            * jnp.asarray(HEAD_DIM**-0.5, LOW)
        )
        place_rows = span(core * half + at, cols, 256)
        keys[place_rows, :] = dot(block, weight[:, width : 2 * width]).astype(LOW)
        values[place_rows, :] = (
            dot(block, weight[:, 2 * width :]) + value_bias[...].astype(F32).reshape(1, -1)
        ).astype(LOW)
        return place_rows

    shares = []
    for step, (rows, at) in enumerate(((here, x * cols), (there, (1 - x) * cols))):
        if step == 1:
            move_tokens.wait_recv()
        place_rows = project(rows, at)
        for i, array in enumerate((keys, values)):
            n = 5 + step * 2 + i
            move = remote(
                array.at[place_rows], array.at[place_rows], send_sems.at[n], recv_sems.at[n], other_core
            )
            move.start()
            shares.append(move)
        hop(1 + step)
    for move in moves:
        move.wait_recv()
    all_ids = jnp.concatenate(
        [ids_in[0], ids_in[2], ids_in[1], ids_in[3]], axis=1
    ).astype(F32)
    column = jnp.broadcast_to(all_ids[0:1, :], (128, 2 * half)).T[:, 0:1]
    own_ids = jnp.concatenate([ids_in[core], ids_in[2 + core]], axis=1).astype(F32)[0:1, :]
    bias[...] = jnp.where(column == own_ids, 0.0, masked_score)
    for i in range(3, len(hops) + 1):
        hop(i)
    own_flag = keep[x].astype(F32)
    scale[...] = own_flag * (float(2 * 8 * far) / counts[len(hops)])
    kept[...] = counts[len(hops)].astype(jnp.int32)
    for move in shares:
        move.wait_recv()

    def pair_step(p, carry):
        pair = span(p * PAIR, PAIR, PAIR)
        values_t[...] = values[:, pair].T
        key_pair = keys[:, pair]
        query_pair = query[:, pair]
        for i in range(2):
            chosen = jnp.where(lanes_of(i, half), query_pair, jnp.zeros_like(query_pair))
            scores = dot_nt(key_pair, chosen) + bias[...]
            top = jnp.max(scores, axis=0, keepdims=True)
            powered = jnp.exp(scores - top)
            total = jnp.sum(powered, axis=0, keepdims=True)
            mixed = dot(values_t[i * HEAD_DIM : (i + 1) * HEAD_DIM, :], powered.astype(LOW))
            attended[span(p * PAIR + i * HEAD_DIM, HEAD_DIM, HEAD_DIM), :] = mixed / total
            log_total[pl.ds(p * 2 + i, 1), :] = top + jnp.log(total)
        return carry

    lax.fori_loop(0, width // PAIR, pair_step, 0)
    move_cot.wait_recv()
    stay_cot.wait()
    for move in [move_tokens, move_cot, *moves, *count_moves, *shares]:
        move.wait_send()


def here_of(x, cols):
    return span(x * cols, cols, 256)


def count_hops(place, far):
    hops = [device_at(place, y=1 - place["y"])]
    hops += [device_at(place, z=flipped(place["z"], bit)) for bit in (1, 2)]
    hops += [device_at(place, far=flipped(place["far"], bit)) for bit in far_bits(far)]
    return hops


def front(tokens, cot, segments, keep, weight, query_bias, value_bias, far):
    _, cols, width = tokens.shape
    half = 2 * cols
    hops = 3 + len(far_bits(far))
    vmem, any_space = pl.BlockSpec(memory_space=pltpu.VMEM), pl.BlockSpec(memory_space=pl.ANY)
    dma = pltpu.SemaphoreType.DMA
    return pl.pallas_call(
        partial(front_kernel, far),
        out_shape=[
            jax.ShapeDtypeStruct((half, width), LOW),
            jax.ShapeDtypeStruct((half, width), LOW),
            jax.ShapeDtypeStruct((half, width), LOW),
            jax.ShapeDtypeStruct((2 * half, width), LOW),
            jax.ShapeDtypeStruct((2 * half, width), LOW),
            jax.ShapeDtypeStruct((width, half), F32),
            jax.ShapeDtypeStruct((16, half), F32),
            jax.ShapeDtypeStruct((2 * half, half), F32),
            jax.ShapeDtypeStruct((8, 128), F32),
            jax.ShapeDtypeStruct((8, 128), jnp.int32),
        ],
        in_specs=[vmem, any_space, vmem, pl.BlockSpec(memory_space=pltpu.SMEM), vmem, vmem, vmem],
        out_specs=[vmem, any_space] + [vmem] * 8,
        scratch_shapes=[
            pltpu.VMEM((2, 8, cols), jnp.int32),
            pltpu.VMEM((4, 8, cols), jnp.int32),
            pltpu.VMEM((hops + 1, 8, 128), F32),
            pltpu.VMEM((hops, 8, 128), F32),
            pltpu.VMEM((PAIR, 2 * half), LOW),
            dma((9,)),
            dma((9,)),
            dma((hops,)),
            dma((hops,)),
            dma(()),
        ],
        compiler_params=pltpu.CompilerParams(
            collective_id=1, has_side_effects=True, vmem_limit_bytes=VMEM_LIMIT
        ),
        name="front",
    )(tokens, cot, segments, keep, weight, query_bias, value_bias)


def middle_kernel(
    attended,
    tokens,
    cot,
    scale,
    out_weight_any,
    up_weight_any,
    down_weight_any,
    out_bias,
    first_gain,
    first_shift,
    up_bias,
    down_bias,
    second_gain,
    second_shift,
    mixed,
    first_in,
    attended_grad,
    delta,
    out_grad,
    up_grad,
    down_grad,
    vectors,
    out_weight,
    up_weight,
    down_weight,
    low,
    low_t,
    work,
    normed,
    inverse,
    first,
    first_low,
    first_t,
    hidden,
    slope,
    second_in,
    ffn_grad,
    load_sems,
):
    width = first.shape[1]
    rows = first.shape[0]
    ff = hidden.shape[1]
    step, tile = 512, 64
    loads = []
    for i, (a, b) in enumerate(
        ((out_weight_any, out_weight), (up_weight_any, up_weight), (down_weight_any, down_weight))
    ):
        loads.append(pltpu.make_async_copy(a, b, load_sems.at[i]))
        loads[-1].start()
    factor = scale[0:1, 0:1]
    low_t[...] = attended[...].astype(LOW)
    low[...] = attended[...].T.astype(LOW)
    loads[0].wait()
    work[...] = dot(low[...], out_weight[...])
    mean = partial(jnp.mean, axis=-1, keepdims=True)

    def tiles(body, carry):
        def one(t, kept):
            return body(span(t * tile, tile, tile), kept)

        return lax.fori_loop(0, rows // tile, one, carry)

    def normalize(values):
        centered = values - mean(values)
        inv = lax.rsqrt(mean(centered * centered) + norm_eps)
        return centered * inv, inv

    def first_norm(at, carry):
        branch = work[at, :] + out_bias[...].astype(F32).reshape(1, -1)
        n, inv = normalize(tokens[at, :].astype(F32) + factor * branch)
        normed[at, :] = n
        inverse[at, :] = jnp.broadcast_to(inv, (tile, 128))
        out = n * first_gain[...].astype(F32).reshape(1, -1) + first_shift[...].astype(F32).reshape(1, -1)
        first[at, :] = out
        first_low[at, :] = out.astype(LOW)
        return carry

    tiles(first_norm, 0)
    first_t[...] = first_low[...].T
    loads[1].wait()
    loads[2].wait()

    def up_step(f, carry):
        cols = span(f * step, step, step)
        pre = dot(first_low[...], up_weight[:, cols]) + up_bias[cols].astype(F32).reshape(1, -1)
        chance = 0.5 + 0.5 * lax.erf(pre * (2.0**-0.5))
        density = jnp.exp(pre * pre * -0.5) * 0.3989422804014327
        hidden[:, cols] = (pre * chance).astype(LOW)
        slope[:, cols] = (chance + pre * density).astype(LOW)
        return carry

    lax.fori_loop(0, ff // step, up_step, 0)
    work[...] = dot(hidden[...], down_weight[...])
    zero = jnp.zeros((1, width), F32)

    def total(values):
        return jnp.sum(values, axis=0, keepdims=True)

    def second_norm(at, carry):
        gain_sum, shift_sum, bias_sum = carry
        gain = second_gain[...].astype(F32).reshape(1, -1)
        n, inv = normalize(first[at, :] + factor * (work[at, :] + down_bias[...].astype(F32).reshape(1, -1)))
        mixed[at, :] = (n * gain + second_shift[...].astype(F32).reshape(1, -1)).astype(LOW)
        grad = cot[at, :].astype(F32)
        scaled = grad * gain
        inner = inv * (scaled - mean(scaled) - n * mean(scaled * n))
        second_in[at, :] = inner
        low_grad = (factor * inner).astype(LOW)
        ffn_grad[at, :] = low_grad
        return (
            gain_sum + total(grad * n),
            shift_sum + total(grad),
            bias_sum + total(low_grad.astype(F32)),
        )

    second_gain_sum, second_shift_sum, down_sum = tiles(second_norm, (zero, zero, zero))
    vectors[...] = jnp.zeros_like(vectors)
    vectors[5:6, :] = down_sum
    vectors[6:7, :] = second_gain_sum
    vectors[7:8, :] = second_shift_sum
    work[...] = jnp.zeros_like(work)

    def down_step(f, carry):
        cols = span(f * step, step, step)
        pulled = dot_nt(ffn_grad[...], down_weight[cols, :])
        pre_grad = (slope[:, cols].astype(F32) * pulled).astype(LOW)
        slope[:, cols] = pre_grad
        down_grad[cols, :] = dot(hidden[:, cols].T, ffn_grad[...]).astype(LOW)
        up_grad[:, cols] = dot(first_t[...], pre_grad).astype(LOW)
        work[...] += dot_nt(pre_grad, up_weight[:, cols])
        return carry

    lax.fori_loop(0, ff // step, down_step, 0)

    for i in range(ff // width):
        vectors[8 + i : 9 + i, :] = total(slope[:, i * width : (i + 1) * width].astype(F32))

    def first_back(at, carry):
        gain_sum, shift_sum, bias_sum = carry
        grad = second_in[at, :] + work[at, :]
        n = normed[at, :]
        scaled = grad * first_gain[...].astype(F32).reshape(1, -1)
        inner = inverse[at, 0:1] * (scaled - mean(scaled) - n * mean(scaled * n))
        first_in[at, :] = inner
        low_grad = (factor * inner).astype(LOW)
        ffn_grad[at, :] = low_grad
        return (
            gain_sum + total(grad * n),
            shift_sum + total(grad),
            bias_sum + total(low_grad.astype(F32)),
        )

    first_gain_sum, first_shift_sum, out_sum = tiles(first_back, (zero, zero, zero))
    vectors[2:3, :] = out_sum
    vectors[3:4, :] = first_gain_sum
    vectors[4:5, :] = first_shift_sum
    branch_grad = ffn_grad[...]
    out_grad[...] = dot(low_t[...], branch_grad).astype(LOW)
    attended_grad[...] = dot_nt(branch_grad, out_weight[...]).astype(LOW)
    product = dot_nt(out_weight[...], branch_grad).astype(LOW).astype(F32) * attended[...]
    delta[...] = jnp.zeros_like(delta)
    for h in range(width // HEAD_DIM):
        delta[h : h + 1, :] = total(product[h * HEAD_DIM : (h + 1) * HEAD_DIM, :])


def middle(attended, tokens, cot, scale, weights, vectors):
    rows, width = tokens.shape
    ff = weights[1].shape[1]
    vmem, any_space = pl.BlockSpec(memory_space=pltpu.VMEM), pl.BlockSpec(memory_space=pl.ANY)
    shape = jax.ShapeDtypeStruct
    return pl.pallas_call(
        middle_kernel,
        out_shape=[
            shape((rows, width), LOW),
            shape((rows, width), F32),
            shape((rows, width), LOW),
            shape((16, rows), F32),
            shape((width, width), LOW),
            shape((width, ff), LOW),
            shape((ff, width), LOW),
            shape((16, width), F32),
        ],
        in_specs=[vmem] * 4 + [any_space] * 3 + [vmem] * 7,
        out_specs=[vmem] * 8,
        scratch_shapes=[
            pltpu.VMEM((width, width), LOW),
            pltpu.VMEM((width, ff), LOW),
            pltpu.VMEM((ff, width), LOW),
            pltpu.VMEM((rows, width), LOW),
            pltpu.VMEM((width, rows), LOW),
            pltpu.VMEM((rows, width), F32),
            pltpu.VMEM((rows, width), F32),
            pltpu.VMEM((rows, 128), F32),
            pltpu.VMEM((rows, width), F32),
            pltpu.VMEM((rows, width), LOW),
            pltpu.VMEM((width, rows), LOW),
            pltpu.VMEM((rows, ff), LOW),
            pltpu.VMEM((rows, ff), LOW),
            pltpu.VMEM((rows, width), F32),
            pltpu.VMEM((rows, width), LOW),
            pltpu.SemaphoreType.DMA((3,)),
        ],
        compiler_params=pltpu.CompilerParams(vmem_limit_bytes=VMEM_LIMIT),
        name="middle",
    )(attended, tokens, cot, scale, *weights, *vectors)


def back_kernel(far, groups, *refs):
    (query, keys, values, grads, log_total, delta, bias, tokens, first_in, weight, vectors) = refs[:11]
    given = dict(zip(("out", "up", "down"), refs[11:14]))
    mixed_row = refs[14]
    names = [m[0] for m in MATRICES]
    whole = dict(zip(names, refs[15:19]))
    vector_out, mixed, tokens_grad = refs[19:22]
    own = dict(zip(names, refs[22:26]))
    chunks = chunks_of(far)
    n = len(chunks)
    inboxes = refs[26 : 26 + n]
    (
        keys_t,
        query_t,
        mine,
        other,
        arrived,
        joined,
        tokens_t,
        row_grad,
        vec_inbox,
        vec_totals,
        send_sems,
        recv_sems,
        vec_send,
        vec_recv,
        load_sems,
        store_sems,
        pair_send,
        pair_recv,
        row_send,
        row_recv,
        local_sems,
    ) = refs[26 + n :]
    place = coordinates()
    x, core = place["x"], place["core"]
    half, width = query.shape
    cols = half // 2
    loads = {}
    for i, chunk in enumerate(chunks):
        if chunk.matrix == "in":
            continue
        rows = 768 + chunk.row_step
        wide = chunk.width + chunk.col_step
        part = (pl.ds(chunk.row, rows), pl.ds(chunk.col, wide))
        loads[i] = pltpu.make_async_copy(
            given[chunk.matrix].at[part], own[chunk.matrix].at[part], load_sems.at[i]
        )
        loads[i].start()
    greet(place, far)
    other_x = device_at(place, x=1 - x)
    other_core = device_at(place, core=1 - core)
    here, there = span(x * cols, cols, 256), span((1 - x) * cols, cols, 256)
    move_mixed = remote(
        mixed_row.at[there], mixed.at[x], row_send.at[0], row_recv.at[0], other_x
    )
    move_mixed.start()
    stay_mixed = pltpu.make_async_copy(mixed_row.at[here], mixed.at[x], local_sems.at[0])
    stay_mixed.start()
    gens = []
    used = [0]

    def begin(i):
        chunk = chunks[i]
        if i in loads:
            loads[i].wait()
        part = pl.ds(used[0], chunk.copies)
        used[0] += chunk.copies
        gen = chunk.steps(
            place,
            own[chunk.matrix],
            whole[chunk.matrix],
            inboxes[i],
            send_sems.at[part],
            recv_sems.at[part],
            store_sems.at[i],
        )
        next(gen)
        gens.append(gen)

    def advance():
        for gen in list(gens):
            try:
                next(gen)
            except StopIteration:
                gens.remove(gen)

    for i in loads:
        begin(i)
    keys_t[...] = keys[...].T
    tokens_t[...] = tokens[...].T

    def one_side(p, side, first):
        pair = span(p * PAIR, PAIR, PAIR)
        at = span(side * half, half, 512)
        key_pair, value_pair = keys[at, pair], values[at, pair]
        query_pair, grad_pair = query[:, pair], grads[:, pair]
        zero = jnp.zeros_like(query_pair)
        key_sum = value_sum = None
        for i in range(2):
            head = pl.ds(p * 2 + i, 1)
            chosen = jnp.where(lanes_of(i, half), query_pair, zero)
            pulled = jnp.where(lanes_of(i, half), grad_pair, zero)
            chance = jnp.exp(dot_nt(key_pair, chosen) + bias[at, :] - log_total[head, :])
            slope = dot_nt(value_pair, pulled) - delta[head, :]
            score_grad = (chance * slope).astype(LOW)
            value_part = dot(chance.astype(LOW), pulled)
            key_part = dot(score_grad, chosen)
            value_sum = value_part if value_sum is None else value_sum + value_part
            key_sum = key_part if key_sum is None else key_sum + key_part
            lines = span(p * PAIR + i * HEAD_DIM, HEAD_DIM, HEAD_DIM)
            query_part = dot(keys_t[lines, at], score_grad)
            if first:
                query_t[lines, :] = query_part
            else:
                query_t[lines, :] += query_part
        return key_sum, value_sum

    def pair_step(p, carry):
        pair = span(p * PAIR, PAIR, PAIR)
        second = span(width + p * PAIR, PAIR, PAIR)
        key_sum, value_sum = one_side(p, 1 - core, True)
        other[:, pair] = key_sum.astype(LOW)
        other[:, second] = value_sum.astype(LOW)
        key_sum, value_sum = one_side(p, core, False)
        mine[:, pair] = key_sum
        mine[:, second] = value_sum
        return carry

    pairs = width // PAIR
    each = pairs // groups
    pair_moves = []
    for g in range(groups):
        lax.fori_loop(g * each, (g + 1) * each, pair_step, 0)
        for i in range(2):
            part = pl.ds(i * width + g * each * PAIR, each * PAIR)
            move = remote(
                other.at[:, part],
                arrived.at[:, part],
                pair_send.at[g * 2 + i],
                pair_recv.at[g * 2 + i],
                other_core,
            )
            move.start()
            pair_moves.append(move)
        advance()
    joined[:, :width] = (query_t[...].T * HEAD_DIM**-0.5).astype(LOW)
    for move in pair_moves:
        move.wait_recv()
    joined[:, width:] = (mine[...] + arrived[...].astype(F32)).astype(LOW)
    for j in range(3):
        part = pl.ds(j * width, width)
        own["in"][:, part] = dot(tokens_t[...], joined[:, part]).astype(LOW)
        begin(5 + j)
    advance()
    vec_totals[0] = vectors[...]
    for i, j in ((0, 0), (1, 2)):
        vec_totals[0, i : i + 1, :] = jnp.sum(
            joined[:, j * width : (j + 1) * width].astype(F32), axis=0, keepdims=True
        )
    gens.append(vector_steps(place, far, vec_totals, vec_inbox, vec_send, vec_recv))
    advance()
    row_grad[...] = (first_in[...] + dot_nt(joined[...], weight[...])).astype(LOW)
    move_grad = remote(
        row_grad.at[there], tokens_grad.at[x], row_send.at[1], row_recv.at[1], other_x
    )
    move_grad.start()
    stay_grad = pltpu.make_async_copy(row_grad.at[here], tokens_grad.at[x], local_sems.at[1])
    stay_grad.start()
    while gens:
        advance()
    vector_out[...] = vec_totals[len(vector_hops(place, far))]
    stay_mixed.wait()
    stay_grad.wait()
    move_mixed.wait()
    move_grad.wait()
    for move in pair_moves:
        move.wait_send()


def back(rows, matrices, mixed_row, far):
    chunks = chunks_of(far)
    groups = 6
    hops = 5 + len(far_bits(far))
    copies = sum(c.copies for c in chunks)
    half, width = rows[0].shape
    vmem, any_space = pl.BlockSpec(memory_space=pltpu.VMEM), pl.BlockSpec(memory_space=pl.ANY)
    dma = pltpu.SemaphoreType.DMA
    shape = jax.ShapeDtypeStruct
    return pl.pallas_call(
        partial(back_kernel, far, groups),
        out_shape=[shape((a, b), LOW) for _, a, b in MATRICES]
        + [shape((16, width), F32), shape((2, half // 2, width), LOW), shape((2, half // 2, width), LOW)],
        in_specs=[vmem] * 11 + [any_space] * 4,
        out_specs=[any_space] * 4 + [vmem] + [any_space] * 2,
        scratch_shapes=[pltpu.VMEM((a, b), LOW) for _, a, b in MATRICES]
        + [pltpu.VMEM((c.received, c.width), LOW) for c in chunks]
        + [
            pltpu.VMEM((width, 2 * half), LOW),
            pltpu.VMEM((width, half), F32),
            pltpu.VMEM((half, 2 * width), F32),
            pltpu.VMEM((half, 2 * width), LOW),
            pltpu.VMEM((half, 2 * width), LOW),
            pltpu.VMEM((half, 3 * width), LOW),
            pltpu.VMEM((width, half), LOW),
            pltpu.VMEM((half, width), LOW),
            pltpu.VMEM((hops, 16, width), F32),
            pltpu.VMEM((hops + 1, 16, width), F32),
            dma((copies,)),
            dma((copies,)),
            dma((hops,)),
            dma((hops,)),
            dma((len(chunks),)),
            dma((len(chunks),)),
            dma((2 * groups,)),
            dma((2 * groups,)),
            dma((2,)),
            dma((2,)),
            dma((2,)),
        ],
        compiler_params=pltpu.CompilerParams(
            collective_id=0, has_side_effects=True, vmem_limit_bytes=VMEM_LIMIT
        ),
        name="back",
    )(*rows, *matrices, mixed_row)


def body(
    tokens,
    segment_ids,
    keep_flags,
    input_weight,
    query_bias,
    value_bias,
    output_weight,
    output_bias,
    first_gain,
    first_shift,
    up_weight,
    up_bias,
    down_weight,
    down_bias,
    second_gain,
    second_shift,
    cotangent,
):
    far = lax.axis_size("batch") // 8
    row_tokens, row_cot, query, keys, values, attended, log_total, bias, scale, kept = front(
        tokens, cotangent, segment_ids, keep_flags, input_weight, query_bias, value_bias, far
    )
    mixed_row, first_in, attended_grad, delta, out_grad, up_grad, down_grad, vectors = middle(
        attended,
        row_tokens,
        row_cot,
        scale,
        (output_weight, up_weight, down_weight),
        (output_bias, first_gain, first_shift, up_bias, down_bias, second_gain, second_shift),
    )
    *low, vectors, mixed, tokens_grad = back(
        (
            query,
            keys,
            values,
            attended_grad,
            log_total,
            delta,
            bias,
            row_tokens,
            first_in,
            input_weight,
            vectors,
        ),
        (out_grad, up_grad, down_grad),
        mixed_row,
        far,
    )
    full = [g.astype(F32) for g in low]
    return (
        mixed,
        tokens_grad,
        kept[0, 0],
        full[0],
        vectors[0],
        vectors[1],
        full[1],
        vectors[2],
        vectors[3],
        vectors[4],
        full[2],
        vectors[8:12].reshape(-1),
        full[3],
        vectors[5],
        vectors[6],
        vectors[7],
    )


def solution(mesh):
    in_specs = (
        P("batch", "blk", None),
        P("batch", "blk"),
        P("batch"),
        P(),
        P(),
        P(),
        P(),
        P(),
        P(),
        P(),
        P(),
        P(),
        P(),
        P(),
        P(),
        P(),
        P("batch", "blk", None),
    )
    out_specs = (
        P("batch", "blk", None),
        P("batch", "blk", None),
        P(),
        P(),
        P(),
        P(),
        P(),
        P(),
        P(),
        P(),
        P(),
        P(),
        P(),
        P(),
        P(),
        P(),
    )
    return jax.shard_map(body, mesh=mesh, in_specs=in_specs, out_specs=out_specs, check_vma=False)
```

```python
from functools import partial
from types import SimpleNamespace

import jax
import jax.numpy as jnp
from jax import lax
from jax.experimental import pallas as pl
from jax.experimental.pallas import tpu as pltpu
from jax.sharding import PartitionSpec as P

HEAD_DIM = 64


masked_score = -1e30
norm_eps = 1e-05


MESH = pl.DeviceIdType.MESH


def coordinates():
    batch, blk = lax.axis_index("batch"), lax.axis_index("blk")
    return dict(
        core=lax.rem(blk, 2),
        x=lax.div(blk, 2),
        y=lax.rem(batch, 2),
        l=lax.rem(lax.div(batch, 2), 2),
        h=lax.rem(lax.div(batch, 4), 2),
        far=lax.div(batch, 8),
    )


def device_at(place, **changes):
    at = SimpleNamespace(**{**place, **changes})
    return (at.far * 8 + at.h * 4 + at.l * 2 + at.y, at.x * 2 + at.core)


def across(place, d):
    return device_at(place, **{d: 1 - place[d]})


def flipped(index, bit):
    return index + bit - 2 * bit * lax.rem(lax.div(index, bit), 2)


def far_bits(far):
    return [1 << b for b in range(far.bit_length() - 1)]


def far_hops(place, far):
    return [device_at(place, far=flipped(place["far"], bit)) for bit in far_bits(far)]


def greet(place, far):
    partners = [across(place, d) for d in ("core", "x", "y", "l", "h")]
    partners += far_hops(place, far)
    partners.append(device_at(place, x=1 - place["x"], core=1 - place["core"]))
    barrier = pltpu.get_barrier_semaphore()
    for partner in partners:
        pl.semaphore_signal(barrier, inc=1, device_id=partner, device_id_type=MESH)
    pl.semaphore_wait(barrier, len(partners))


class Chunk:
    def __init__(self, matrix, row, row_step, col, col_step, width, order, far):
        self.matrix, self.width, self.order, self.far = matrix, width, order, far
        self.row, self.row_step, self.col, self.col_step = row, row_step, col, col_step
        self.share = 768 >> len(order)
        self.received = 768 - self.share + self.share * len(far_bits(far))
        self.copies = 2 + 2 * len(order) + len(far_bits(far))

    def region(self, ref, half, row, rows):
        row = self.row + half * self.row_step + row
        col = self.col + half * self.col_step
        return ref.at[
            pl.ds(pl.multiple_of(row, 16), rows), pl.ds(pl.multiple_of(col, 128), self.width)
        ]

    def steps(self, place, own, whole, core_box, inbox, send_sems, recv_sems, store_sem):
        sent = []

        def send(source, target, device):
            i = len(sent)
            copy = pltpu.make_async_remote_copy(
                src_ref=source,
                dst_ref=target,
                send_sem=send_sems.at[i],
                recv_sem=recv_sems.at[i],
                device_id=device,
                device_id_type=MESH,
            )
            copy.start()
            sent.append(copy)
            return copy

        def add(row, rows, froms, inbox=inbox):
            tile = min(rows, 48)

            def one(t, carry):
                at = pl.multiple_of(t * tile, 16)
                here = self.region(own, core, row + at, tile)
                total = here[...].astype(jnp.float32)
                for start in froms:
                    total = total + inbox[pl.ds(pl.multiple_of(start + at, 16), tile), :].astype(
                        jnp.float32
                    )
                here[...] = total.astype(jnp.bfloat16)
                return carry

            lax.fori_loop(0, rows // tile, one, 0)

        core = place["core"]
        copy = send(
            self.region(own, 1 - core, 0, 768),
            core_box,
            device_at(place, core=1 - core),
        )
        yield
        copy.wait_recv()
        add(0, 768, (0,), core_box)
        yield
        row, rows, used = 0, 768, 0
        for d in self.order:
            rows //= 2
            copy = send(
                self.region(own, core, row + (1 - place[d]) * rows, rows),
                inbox.at[pl.ds(used, rows)],
                across(place, d),
            )
            row = row + place[d] * rows
            yield
            copy.wait_recv()
            add(row, rows, (used,))
            used += rows
            yield
        for device in far_hops(place, self.far):
            copy = send(self.region(own, core, row, rows), inbox.at[pl.ds(used, rows)], device)
            yield
            copy.wait_recv()
            copy.wait_send()
            sent[-1] = None
            add(row, rows, (used,))
            used += rows
        store = pltpu.make_async_copy(
            self.region(own, core, row, rows), self.region(whole, core, row, rows), store_sem
        )
        store.start()
        source = own
        for d in reversed(self.order):
            copy = send(
                self.region(source, core, row, rows),
                self.region(whole, core, row, rows),
                across(place, d),
            )
            yield
            copy.wait_recv()
            if source is own:
                store.wait()
            source = whole
            row = row - place[d] * rows
            rows *= 2
            yield
        copy = send(
            self.region(whole, core, 0, 768),
            self.region(whole, core, 0, 768),
            device_at(place, core=1 - core),
        )
        yield
        copy.wait_recv()
        yield
        for copy in sent:
            if copy is not None:
                copy.wait_send()


def vector_hops(place, far):
    return [across(place, d) for d in ("core", "x", "y", "l", "h")] + far_hops(place, far)


def vector_steps(place, far, totals, inbox, send_sems, recv_sems):
    sent = []
    for i, device in enumerate(vector_hops(place, far)):
        copy = pltpu.make_async_remote_copy(
            src_ref=totals.at[i],
            dst_ref=inbox.at[i],
            send_sem=send_sems.at[i],
            recv_sem=recv_sems.at[i],
            device_id=device,
            device_id_type=MESH,
        )
        copy.start()
        sent.append(copy)
        yield
        copy.wait_recv()
        totals[i + 1] = totals[i] + inbox[i]
        yield
    for copy in sent:
        copy.wait_send()


LINKS = ("yxlh", "xylh", "lyxh", "xylh", "lyhx", "lxyh", "xylh", "yxlh", "lyxh", "xlyh", "yxlh", "yxlh")
PLAN = (
    13, 0, 4, 14, 1, 5, 15, 0, 6, 4, 4, 0, 2, 16, 1, 1, 5, 7, 6, 6, 2, 5, 3, 2, 17, 7, 7, 3,
    8, 0, 18, 19, 4, 20, 8, 3, 8, 21, 4, 22, 0, 23, 1, 7, 1, 24, 6, 25, 4, 4, 6, 26, 5, 7, 2, 9,
    1, 1, 5, 2, 27, 0, 0, 28, 3, 3, 4, 6, 6, 9, 8, 29, 1, 1, 9, 4, 30, 0, 0, 2, 8, 2, 31, 6,
    10, 1, 1, 7, 7, 5, 6, 3, 5, 4, 4, 32, 0, 11, 8, 0, 10, 10, 2, 8, 3, 2, 12, 33, 11, 1, 1, 7,
    7, 4, 4, 6, 9, 5, 0, 12, 12, 8, 3, 2, 11, 6, 9, 10, 10, 12, 7, 0, 8, 1, 1, 5, 6, 4, 6, 7,
    3, 11, 11, 8, 12, 4, 9, 8, 0, 0, 5, 5, 1, 10, 10, 12, 1, 9, 7, 7, 6, 12, 3, 3, 6, 11, 4, 11,
    8, 5, 8, 10, 10, 9, 5, 9, 3, 3, 0, 0, 12, 12, 6, 6, 2, 4, 7, 5, 10, 10, 8, 9, 11, 11, 7, 12,
    9, 2, 8, 3, 1, 1, 10, 10, 0, 0, 3, 11, 11, 9, 2, 1, 8, 8, 9, 0, 5, 7, 7, 10, 10, 11, 11, 3,
    6, 6, 9, 9, 2, 4, 4, 3, 6, 2, 5, 5, 4, 11, 11, 7, 7, 10, 10, 2, 2, 7, 9, 9, 8, 8, 11, 11,
    3, 3, 8, 10, 10, 3, 10, 5, 5, 9, 9, 2, 2, 11, 11, 5, 9, 2, 11,
)


def chunks_of(far):
    parts = [("down", j * 768, 0) for j in range(4)] + [("up", 0, j * 768) for j in range(4)]
    parts += [("out", 0, 0)]
    chunks = [
        Chunk(matrix, row, 0, col, 384, 384, links, far)
        for (matrix, row, col), links in zip(parts, LINKS)
    ]
    for (col, step), links in zip(((0, 768), (1536, 384), (384, 768)), LINKS[9:]):
        chunks.append(Chunk("into", 0, 0, col, step, 384, links, far))
    return chunks


F32, LOW = jnp.float32, jnp.bfloat16
PAIR = 2 * HEAD_DIM
VMEM_LIMIT = 62 << 20


def dot(left, right):
    return lax.dot_general(left, right, (((1,), (0,)), ((), ())), preferred_element_type=F32)


def dot_nt(left, right):
    return lax.dot_general(left, right, (((1,), (1,)), ((), ())), preferred_element_type=F32)


def span(start, size, unit):
    return pl.ds(pl.multiple_of(start, unit), size)


def lanes_of(i, rows):
    lane = lax.broadcasted_iota(jnp.int32, (rows, PAIR), 1)
    return lax.div(lane, HEAD_DIM) == i


def remote(source, target, send_sem, recv_sem, device):
    return pltpu.make_async_remote_copy(
        src_ref=source,
        dst_ref=target,
        send_sem=send_sem,
        recv_sem=recv_sem,
        device_id=device,
        device_id_type=MESH,
    )


def here_of(x, cols):
    return span(x * cols, cols, 256)


def count_hops(place, far):
    return [across(place, d) for d in ("y", "l", "h")] + far_hops(place, far)


def layer_kernel(far, names, *refs):
    r = SimpleNamespace(**dict(zip(names, refs)))
    extra = refs[len(names) :]
    r.boxes, r.core_boxes = extra[: len(extra) - 9], extra[len(extra) - 9 :]
    place = coordinates()
    x, core = place["x"], place["core"]
    half, width = r.row_tokens.shape
    cols = half // 2
    ff = r.hidden.shape[1]
    tile = 64
    chunks = chunks_of(far)
    n = len(chunks)
    boxes = [r.boxes[i] for i in range(n)]
    core_boxes = [r.core_boxes[i] for i in range(9)]
    core_boxes += [r.up_weight.at[:, pl.ds(3 * width + i * 384, 384)] for i in range(2)]
    core_boxes.append(r.down_weight.at[pl.ds(3 * width, width), pl.ds(0, 384)])
    own = dict(down=r.down_own, up=r.up_own, out=r.out_own, into=r.up_weight)
    whole = dict(down=r.down_whole, up=r.up_whole, out=r.out_whole, into=r.into_whole)
    other_x = device_at(place, x=1 - x)
    other_core = device_at(place, core=1 - core)
    here, there = here_of(x, cols), here_of(1 - x, cols)
    row_tokens, row_cot = r.row_tokens, r.row_cot
    query, keys, values, bias = r.query, r.keys, r.values, r.bias
    attended, log_total = r.attended, r.log_total
    in_first, in_later = r.down_own, r.down_weight
    out_weight, up_weight, down_weight = r.out_weight, r.up_weight, r.down_weight

    def local(source, target, sem):
        copy = pltpu.make_async_copy(source, target, sem)
        copy.start()
        return copy

    def load_in(target, sems):
        return [
            local(
                r.into_any.at[:, pl.ds(j * width, width)],
                target.at[pl.ds(j * width, width), :],
                sems.at[j],
            )
            for j in range(3)
        ]

    stay_tokens = local(r.tokens_any.at[x], row_tokens.at[here], r.stay_sems.at[0])
    in_loads = load_in(in_first, r.in_sems)
    stay_cot = local(r.cot_any.at[x], row_cot.at[here], r.stay_sems.at[1])
    weight_loads = [
        local(a, b, r.load_sems.at[i])
        for i, (a, b) in enumerate(
            (
                (r.out_any, r.out_weight),
                (r.up_any, r.up_weight),
                (r.down_any, r.down_weight),
            )
        )
    ]
    greet(place, far)
    row_send, row_recv = r.row_send, r.row_recv
    move_tokens = remote(
        r.tokens_any.at[1 - x], row_tokens.at[here], row_send.at[0], row_recv.at[0], other_x
    )
    move_tokens.start()
    ids_out, ids_in = r.ids_out, r.ids_in
    for i in range(2):
        ids_out[i] = jnp.broadcast_to(r.segments[i : i + 1, :], (8, cols))
    blk = x * 2 + core
    moves = []
    for i, (dx, dc) in enumerate(((0, 1), (1, 0), (1, 1))):
        to_x = x + dx - 2 * dx * x
        to_core = core + dc - 2 * dc * core
        moves.append(
            remote(
                ids_out.at[to_x],
                ids_in.at[blk],
                r.id_send.at[i],
                r.id_recv.at[i],
                device_at(place, x=to_x, core=to_core),
            )
        )
        moves[-1].start()
    ids_in[blk] = ids_out[x]
    counts, count_in, keep = r.counts, r.count_in, r.keep
    counts[0] = jnp.full((8, 128), (keep[0] + keep[1]).astype(F32), F32)
    hops = count_hops(place, far)
    count_moves = []

    def hop(i):
        if i:
            count_moves[-1].wait_recv()
            counts[i] = counts[i - 1] + count_in[i - 1]
        if i < len(hops):
            move = remote(
                counts.at[i], count_in.at[i], r.count_send.at[i], r.count_recv.at[i], hops[i]
            )
            move.start()
            count_moves.append(move)

    hop(0)
    move_cot = remote(
        r.cot_any.at[1 - x], row_cot.at[here], row_send.at[1], row_recv.at[1], other_x
    )

    def as_row(ref, part=slice(None)):
        return ref[part].astype(F32).reshape(1, -1)

    def project(rows, at):
        block = row_tokens[rows, :]
        place_rows = span(core * half + at, cols, 256)
        keys[place_rows, :] = dot(block, in_first[width : 2 * width, :]).astype(LOW)
        values[place_rows, :] = (
            dot(block, in_first[2 * width : 3 * width, :]) + as_row(r.value_bias)
        ).astype(LOW)
        return place_rows

    def project_query(rows):
        block = row_tokens[rows, :]
        query[rows, :] = (dot(block, in_first[:width, :]) + as_row(r.query_bias)).astype(
            LOW
        ) * jnp.asarray(HEAD_DIM**-0.5, LOW)

    shares = []
    stay_tokens.wait()
    for load in in_loads:
        load.wait()
    for step, (rows, at) in enumerate(((here, x * cols), (there, (1 - x) * cols))):
        if step == 1:
            move_tokens.wait_recv()
            move_cot.start()
        place_rows = project(rows, at)
        for i, array in enumerate((keys, values)):
            k = step * 2 + i
            move = remote(
                array.at[place_rows],
                array.at[place_rows],
                r.share_send.at[k],
                r.share_recv.at[k],
                other_core,
            )
            move.start()
            shares.append(move)
        project_query(rows)
        hop(1 + step)
    for move in moves:
        move.wait_recv()
    all_ids = jnp.concatenate([ids_in[0], ids_in[2], ids_in[1], ids_in[3]], axis=1).astype(F32)
    column = jnp.broadcast_to(all_ids[0:1, :], (128, 2 * half)).T[:, 0:1]
    own_ids = jnp.concatenate([ids_in[core], ids_in[2 + core]], axis=1).astype(F32)[0:1, :]
    bias[...] = jnp.where(column == own_ids, 0.0, masked_score).astype(LOW)
    for i in range(3, len(hops) + 1):
        hop(i)
    factor = keep[x].astype(F32) * (float(2 * 8 * far) / counts[len(hops)])[0:1, 0:1]
    r.kept[...] = counts[len(hops)].astype(jnp.int32)
    for move in shares:
        move.wait_recv()

    def attend(p, carry):
        pair = span(p * PAIR, PAIR, PAIR)
        values_t = values[:, pair].T
        key_pair = keys[:, pair]
        query_pair = query[:, pair]
        for i in range(2):
            chosen = jnp.where(lanes_of(i, half), query_pair, jnp.zeros_like(query_pair))
            scores = dot_nt(key_pair, chosen) + bias[...].astype(F32)
            top = jnp.max(scores, axis=0, keepdims=True)
            powered = jnp.exp(scores - top)
            total = jnp.sum(powered, axis=0, keepdims=True)
            mixture = dot(values_t[i * HEAD_DIM : (i + 1) * HEAD_DIM, :], powered.astype(LOW))
            attended[span(p * PAIR + i * HEAD_DIM, HEAD_DIM, HEAD_DIM), :] = mixture / total
            log_total[pl.ds(p * 2 + i, 1), :] = top + jnp.log(total)
        return carry

    lax.fori_loop(0, width // PAIR, attend, 0)

    low, low_t, work, normed = r.low, r.low_t, r.work, r.normed
    inverse, first, first_low, first_t = r.inverse, r.first, r.first_low, r.first_t
    hidden, slope, vectors = r.hidden, r.slope, r.vec_totals.at[0]
    second_in, ffn_grad, attended_grad = first, first_low, low
    low_t[...] = attended[...].astype(LOW)
    low[...] = attended[...].T.astype(LOW)
    weight_loads[0].wait()
    work[...] = dot(low[...], out_weight[...])
    mean = partial(jnp.mean, axis=-1, keepdims=True)

    def tiles(step, carry):
        def one(t, kept):
            return step(span(t * tile, tile, tile), kept)

        return lax.fori_loop(0, half // tile, one, carry)

    def normalize(given):
        centered = given - mean(given)
        inv = lax.rsqrt(mean(centered * centered) + norm_eps)
        return centered * inv, inv

    def total_of(given):
        return jnp.sum(given, axis=0, keepdims=True)

    def first_norm(at, carry):
        branch = work[at, :] + as_row(r.out_bias)
        unit, inv = normalize(row_tokens[at, :].astype(F32) + factor * branch)
        normed[at, :] = unit
        inverse[at, :] = jnp.broadcast_to(inv, (tile, 128))
        out = unit * as_row(r.first_gain) + as_row(r.first_shift)
        first[at, :] = out
        first_low[at, :] = out.astype(LOW)
        return carry

    tiles(first_norm, 0)
    first_t[...] = first_low[...].T
    weight_loads[1].wait()

    def up_step(f, carry):
        at = span(f * 512, 512, 512)
        pre = dot(first_low[...], up_weight[:, at]) + as_row(r.up_bias, at)
        chance = 0.5 + 0.5 * lax.erf(pre * (2.0**-0.5))
        density = jnp.exp(pre * pre * -0.5) * 0.3989422804014327
        hidden[:, at] = (pre * chance).astype(LOW)
        slope[:, at] = (chance + pre * density).astype(LOW)
        return carry

    lax.fori_loop(0, ff // 512, up_step, 0)
    weight_loads[2].wait()
    work[...] = dot(hidden[...], down_weight[...])
    zero = jnp.zeros((1, width), F32)
    move_cot.wait_recv()
    stay_cot.wait()

    def second_norm(at, carry):
        gain_sum, shift_sum, bias_sum = carry
        gain = as_row(r.second_gain)
        unit, inv = normalize(first[at, :] + factor * (work[at, :] + as_row(r.down_bias)))
        grad = row_cot[at, :].astype(F32)
        row_cot[at, :] = (unit * gain + as_row(r.second_shift)).astype(LOW)
        scaled = grad * gain
        inner = inv * (scaled - mean(scaled) - unit * mean(scaled * unit))
        second_in[at, :] = inner
        low_grad = (factor * inner).astype(LOW)
        ffn_grad[at, :] = low_grad
        return (
            gain_sum + total_of(grad * unit),
            shift_sum + total_of(grad),
            bias_sum + total_of(low_grad.astype(F32)),
        )

    second_gain_sum, second_shift_sum, down_sum = tiles(second_norm, (zero, zero, zero))
    vectors[...] = jnp.zeros_like(vectors)
    vectors[5:6, :] = down_sum
    vectors[6:7, :] = second_gain_sum
    vectors[7:8, :] = second_shift_sum
    mixed, tokens_grad = r.mixed, r.tokens_grad
    move_mixed = remote(row_cot.at[there], mixed.at[x], row_send.at[2], row_recv.at[2], other_x)
    move_mixed.start()
    stay_mixed = local(row_cot.at[here], mixed.at[x], r.stay_sems.at[2])

    offsets = [sum(c.copies for c in chunks[:i]) for i in range(n)]
    gens = {}

    def advance(i):
        if i == n and i not in gens:
            gens[i] = vector_steps(place, far, r.vec_totals, r.vec_inbox, r.vec_send, r.vec_recv)
        if i not in gens:
            part = pl.ds(offsets[i], chunks[i].copies)
            gens[i] = chunks[i].steps(
                place,
                own[chunks[i].matrix],
                whole[chunks[i].matrix],
                core_boxes[i],
                boxes[i],
                r.send_sems.at[part],
                r.recv_sems.at[part],
                r.store_sems.at[i],
            )
        next(gens[i], None)

    def feed_back(f):
        at = pl.ds(f * width, width)
        pulled = dot_nt(ffn_grad[...], down_weight[at, :])
        pre_grad = (slope[:, at].astype(F32) * pulled).astype(LOW)
        slope[:, at] = pre_grad
        own["down"][at, :] = dot(hidden[:, at].T, ffn_grad[...]).astype(LOW)
        own["up"][:, at] = dot(first_t[...], pre_grad).astype(LOW)
        part = dot_nt(pre_grad, up_weight[:, at])
        if f:
            work[...] += part
        else:
            work[...] = part
        vectors[8 + f : 9 + f, :] = total_of(pre_grad.astype(F32))

    tokens_t, delta = first_t, r.delta
    in_again = []

    def first_back(at, carry):
        gain_sum, shift_sum, bias_sum = carry
        grad = second_in[at, :] + work[at, :]
        unit = normed[at, :]
        scaled = grad * as_row(r.first_gain)
        inner = inverse[at, 0:1] * (scaled - mean(scaled) - unit * mean(scaled * unit))
        work[at, :] = inner
        low_grad = (factor * inner).astype(LOW)
        ffn_grad[at, :] = low_grad
        return (
            gain_sum + total_of(grad * unit),
            shift_sum + total_of(grad),
            bias_sum + total_of(low_grad.astype(F32)),
        )

    def norm_back():
        in_again.extend(load_in(in_later, r.in_sems))
        first_gain_sum, first_shift_sum, out_sum = tiles(first_back, (zero, zero, zero))
        vectors[2:3, :] = out_sum
        vectors[3:4, :] = first_gain_sum
        vectors[4:5, :] = first_shift_sum
        branch_grad = ffn_grad[...]
        own["out"][...] = dot(low_t[...], branch_grad).astype(LOW)
        attended_grad[...] = dot_nt(branch_grad, out_weight[...]).astype(LOW)
        product = dot_nt(out_weight[...], branch_grad).astype(LOW).astype(F32) * attended[...]
        delta[...] = jnp.zeros_like(delta)
        for h in range(width // HEAD_DIM):
            delta[h : h + 1, :] = total_of(product[h * HEAD_DIM : (h + 1) * HEAD_DIM, :])
        tokens_t[...] = row_tokens[...].T

    query_t, joined, other, arrived = attended, hidden, slope, r.arrived
    mine = (normed, first)
    pair_moves = []

    def one_side(p, side, fresh):
        pair = pl.ds(p * PAIR, PAIR)
        at = span(side * half, half, 512)
        key_pair, value_pair = keys[at, pair], values[at, pair]
        keys_t = key_pair.T
        query_pair, grad_pair = query[:, pair], attended_grad[:, pair]
        none = jnp.zeros_like(query_pair)
        key_sum = value_sum = None
        for i in range(2):
            head = pl.ds(p * 2 + i, 1)
            chosen = jnp.where(lanes_of(i, half), query_pair, none)
            pulled = jnp.where(lanes_of(i, half), grad_pair, none)
            scores = dot_nt(key_pair, chosen) + bias[at, :].astype(F32)
            chance = jnp.exp(scores - log_total[head, :])
            pull = dot_nt(value_pair, pulled) - delta[head, :]
            score_grad = (chance * pull).astype(LOW)
            value_part = dot(chance.astype(LOW), pulled)
            key_part = dot(score_grad, chosen)
            value_sum = value_part if value_sum is None else value_sum + value_part
            key_sum = key_part if key_sum is None else key_sum + key_part
            lines = pl.ds(p * PAIR + i * HEAD_DIM, HEAD_DIM)
            query_part = dot(keys_t[i * HEAD_DIM : (i + 1) * HEAD_DIM, :], score_grad)
            if fresh:
                query_t[lines, :] = query_part
            else:
                query_t[lines, :] += query_part
        return key_sum, value_sum

    def attend_back(p, mine_too):
        pair = pl.ds(p * PAIR, PAIR)
        if mine_too:
            key_sum, value_sum = one_side(p, core, False)
            mine[0][:, pair] = key_sum
            mine[1][:, pair] = value_sum
            return
        for i, part in enumerate(one_side(p, 1 - core, True)):
            at = pl.ds(i * width + p * PAIR, PAIR)
            other[:, at] = part.astype(LOW)
            k = p * 2 + i
            move = remote(
                other.at[:, at],
                arrived.at[:, at],
                r.pair_send.at[k],
                r.pair_recv.at[k],
                other_core,
            )
            move.start()
            pair_moves.append(move)

    def join(j, at):
        to = pl.ds(j * width + at.start, at.size)
        if j == 0:
            joined[:, to] = (query_t[at, :].T * HEAD_DIM**-0.5).astype(LOW)
        else:
            sent = pl.ds((j - 1) * width + at.start, at.size)
            joined[:, to] = (mine[j - 1][:, at] + arrived[:, sent].astype(F32)).astype(LOW)
        own["into"][:, to] = dot(tokens_t[...], joined[:, to]).astype(LOW)

    def wait_pairs(start, stop):
        for move in pair_moves[2 * start : 2 * stop]:
            move.wait_recv()

    some, rest, every = pl.ds(0, width // 2), pl.ds(width // 2, width // 2), pl.ds(0, width)
    pairs = width // PAIR

    def join_some():
        wait_pairs(0, pairs // 2)
        join(0, some)
        join(1, some)

    def join_values():
        wait_pairs(pairs // 2, pairs)
        join(2, every)

    def join_rest():
        join(0, rest)
        join(1, rest)
        for i, j in ((0, 0), (1, 2)):
            vectors[i : i + 1, :] = total_of(joined[:, j * width : (j + 1) * width].astype(F32))

    row_grad = slope.at[:, pl.ds(2 * width, width)]
    last_moves = []

    def finish_rows():
        for load in in_again:
            load.wait()
        total = work[...]
        for j in range(3):
            at = pl.ds(j * width, width)
            total = total + dot_nt(joined[:, at], in_later[at, :])
        row_grad[...] = total.astype(LOW)
        last_moves.append(
            remote(row_grad.at[there], tokens_grad.at[x], row_send.at[3], row_recv.at[3], other_x)
        )
        last_moves[0].start()
        last_moves.append(local(row_grad.at[here], tokens_grad.at[x], r.stay_sems.at[3]))

    halves = [partial(attend_back, p, side) for p in range(pairs) for side in (False, True)]
    pieces = [partial(feed_back, f) for f in range(ff // width)] + [norm_back]
    pieces += [*halves[:8], join_some, *halves[8:], join_values, join_rest, finish_rows]
    for turn in PLAN:
        if turn <= n:
            advance(turn)
        else:
            pieces[turn - n - 1]()
    for i in range(n + 1):
        for _ in gens[i]:
            pass
    r.vector_out[...] = r.vec_totals[len(vector_hops(place, far))]
    stay_mixed.wait()
    move_mixed.wait()
    for move in last_moves:
        move.wait()
    for move in [move_tokens, move_cot, *moves, *count_moves, *shares, *pair_moves]:
        move.wait_send()


def layer(tokens, cot, segments, keep, weights, vectors, far):
    _, cols, width = tokens.shape
    half = 2 * cols
    ff = weights[2].shape[1]
    chunks = chunks_of(far)
    hops = 5 + len(far_bits(far))
    counts = 3 + len(far_bits(far))
    copies = sum(c.copies for c in chunks)
    vmem, any_space = pl.BlockSpec(memory_space=pltpu.VMEM), pl.BlockSpec(memory_space=pl.ANY)
    smem = pl.BlockSpec(memory_space=pltpu.SMEM)
    shape = jax.ShapeDtypeStruct

    def dma(count):
        return pltpu.SemaphoreType.DMA((count,))

    inputs = dict(
        tokens_any=(tokens, any_space),
        cot_any=(cot, any_space),
        segments=(segments, vmem),
        keep=(keep, smem),
        into_any=(weights[0], any_space),
        out_any=(weights[1], any_space),
        up_any=(weights[2], any_space),
        down_any=(weights[3], any_space),
        **{k: (v, vmem) for k, v in vectors.items()},
    )
    outputs = dict(
        into_whole=(shape((width, 3 * width), LOW), any_space),
        out_whole=(shape((width, width), LOW), any_space),
        up_whole=(shape((width, ff), LOW), any_space),
        down_whole=(shape((ff, width), LOW), any_space),
        vector_out=(shape((16, width), F32), vmem),
        mixed=(shape(tokens.shape, LOW), any_space),
        tokens_grad=(shape(tokens.shape, LOW), any_space),
        kept=(shape((8, 128), jnp.int32), vmem),
    )
    scratch = dict(
        out_weight=((width, width), LOW),
        up_weight=((width, ff), LOW),
        down_weight=((ff, width), LOW),
        out_own=((width, width), LOW),
        up_own=((width, ff), LOW),
        down_own=((ff, width), LOW),
        row_tokens=((half, width), LOW),
        row_cot=((half, width), LOW),
        query=((half, width), LOW),
        keys=((2 * half, width), LOW),
        values=((2 * half, width), LOW),
        bias=((2 * half, half), LOW),
        attended=((width, half), F32),
        log_total=((16, half), F32),
        delta=((16, half), F32),
        low=((half, width), LOW),
        low_t=((width, half), LOW),
        work=((half, width), F32),
        normed=((half, width), F32),
        inverse=((half, 128), F32),
        first=((half, width), F32),
        first_low=((half, width), LOW),
        first_t=((width, half), LOW),
        hidden=((half, ff), LOW),
        slope=((half, ff), LOW),
        arrived=((half, 2 * width), LOW),
        ids_out=((2, 8, cols), jnp.int32),
        ids_in=((4, 8, cols), jnp.int32),
        counts=((counts + 1, 8, 128), F32),
        count_in=((counts, 8, 128), F32),
        vec_inbox=((hops, 16, width), F32),
        vec_totals=((hops + 1, 16, width), F32),
    )
    sems = dict(
        in_sems=3,
        load_sems=3,
        stay_sems=4,
        row_send=4,
        row_recv=4,
        id_send=3,
        id_recv=3,
        count_send=counts,
        count_recv=counts,
        share_send=4,
        share_recv=4,
        pair_send=2 * width // PAIR,
        pair_recv=2 * width // PAIR,
        send_sems=copies,
        recv_sems=copies,
        store_sems=len(chunks),
        vec_send=hops,
        vec_recv=hops,
    )
    boxes = [((c.received, c.width), LOW) for c in chunks]
    boxes += [((width, c.width), LOW) for c in chunks[:9]]
    names = [*inputs, *outputs, *scratch, *sems]
    return pl.pallas_call(
        partial(layer_kernel, far, names),
        out_shape=[o[0] for o in outputs.values()],
        in_specs=[i[1] for i in inputs.values()],
        out_specs=[o[1] for o in outputs.values()],
        scratch_shapes=[pltpu.VMEM(a, t) for a, t in scratch.values()]
        + [dma(c) for c in sems.values()]
        + [pltpu.VMEM(a, t) for a, t in boxes],
        compiler_params=pltpu.CompilerParams(
            collective_id=0, has_side_effects=True, vmem_limit_bytes=VMEM_LIMIT
        ),
        name="layer",
    )(*[i[0] for i in inputs.values()])


def finish_kernel(*refs):
    given, (vectors, kept, mixed, tokens_grad), outs = refs[:4], refs[4:8], refs[8:12]
    (query_b, value_b, out_b, first_g, first_s, up_b, down_b, second_g, second_s) = refs[12:21]
    kept_out, mixed_out, tokens_out = refs[21:24]
    low, wide, load_sems, store_sems, row_sems = refs[24:28], refs[28:32], *refs[32:35]
    held = refs[35:37]
    rows_in = [
        pltpu.make_async_copy(a, b, row_sems.at[i])
        for i, (a, b) in enumerate(zip((mixed, tokens_grad), held))
    ]
    rows_out = [
        pltpu.make_async_copy(a, b, row_sems.at[2 + i])
        for i, (a, b) in enumerate(zip(held, (mixed_out, tokens_out)))
    ]
    tiles = []
    for m, ref in enumerate(given):
        height = 196608 // ref.shape[1] // 16 * 16
        height = next(h for h in range(height, 0, -16) if ref.shape[0] % h == 0)
        tiles += [(m, pl.ds(at, height)) for at in range(0, ref.shape[0], height)]
    loads = [
        pltpu.make_async_copy(given[m].at[at], low[m].at[at], load_sems.at[i])
        for i, (m, at) in enumerate(tiles)
    ]
    stores = [
        pltpu.make_async_copy(wide[m].at[at], outs[m].at[at], store_sems.at[i])
        for i, (m, at) in enumerate(tiles)
    ]
    for load in loads:
        load.start()
    for row in rows_in:
        row.start()
    small = (query_b, value_b, out_b, first_g, first_s, down_b, second_g, second_s)
    kept_out[...] = kept[0:1, 0:1].reshape((1,))
    for i, ref in enumerate(small):
        ref[...] = vectors[i : i + 1, :].reshape(ref.shape)
    width = vectors.shape[1]
    for i in range(up_b.shape[0] // width):
        up_b[pl.ds(i * width, width)] = vectors[8 + i : 9 + i, :].reshape((width,))
    for load, store, (m, at) in zip(loads, stores, tiles):
        load.wait()
        piece = 32 if at.size % 32 == 0 else 16

        def convert(t, carry):
            part = span(at.start + t * piece, piece, 16)
            wide[m][part, :] = low[m][part, :].astype(F32)
            return carry

        lax.fori_loop(0, at.size // piece, convert, 0)
        store.start()
    for row_in, row_out in zip(rows_in, rows_out):
        row_in.wait()
        row_out.start()
    for copy in [*stores, *rows_out]:
        copy.wait()


def finish(matrices, vectors, kept, mixed, tokens_grad):
    width = vectors.shape[1]
    ff = matrices[2].shape[1]
    vmem, any_space = pl.BlockSpec(memory_space=pltpu.VMEM), pl.BlockSpec(memory_space=pl.ANY)
    shape = jax.ShapeDtypeStruct
    sizes = [width, width, width, width, width, ff, width, width, width]
    return pl.pallas_call(
        finish_kernel,
        out_shape=[shape(m.shape, F32) for m in matrices]
        + [shape((k,), F32) for k in sizes]
        + [shape((1,), jnp.int32), shape(mixed.shape, LOW), shape(tokens_grad.shape, LOW)],
        in_specs=[any_space] * 4 + [vmem] * 2 + [any_space] * 2,
        out_specs=[any_space] * 4 + [vmem] * 10 + [any_space] * 2,
        scratch_shapes=[pltpu.VMEM(m.shape, LOW) for m in matrices]
        + [pltpu.VMEM(m.shape, F32) for m in matrices]
        + [
            pltpu.SemaphoreType.DMA((64,)),
            pltpu.SemaphoreType.DMA((64,)),
            pltpu.SemaphoreType.DMA((4,)),
            pltpu.VMEM(mixed.shape, LOW),
            pltpu.VMEM(tokens_grad.shape, LOW),
        ],
        compiler_params=pltpu.CompilerParams(vmem_limit_bytes=VMEM_LIMIT),
        name="finish",
    )(*matrices, vectors, kept, mixed, tokens_grad)


def body(
    tokens,
    segment_ids,
    keep_flags,
    input_weight,
    query_bias,
    value_bias,
    output_weight,
    output_bias,
    first_gain,
    first_shift,
    up_weight,
    up_bias,
    down_weight,
    down_bias,
    second_gain,
    second_shift,
    cotangent,
):
    far = lax.axis_size("batch") // 8
    *low, vectors, mixed, tokens_grad, kept = layer(
        tokens,
        cotangent,
        segment_ids,
        keep_flags,
        (input_weight, output_weight, up_weight, down_weight),
        dict(
            query_bias=query_bias,
            value_bias=value_bias,
            out_bias=output_bias,
            first_gain=first_gain,
            first_shift=first_shift,
            up_bias=up_bias,
            down_bias=down_bias,
            second_gain=second_gain,
            second_shift=second_shift,
        ),
        far,
    )
    into, out, up, down, *small, kept, mixed, tokens_grad = finish(
        low, vectors, kept, mixed, tokens_grad
    )
    query_b, value_b, out_b, first_g, first_s, up_b, down_b, second_g, second_s = small
    return (
        mixed,
        tokens_grad,
        kept.reshape(()),
        into,
        query_b,
        value_b,
        out,
        out_b,
        first_g,
        first_s,
        up,
        up_b,
        down,
        down_b,
        second_g,
        second_s,
    )


def solution(mesh):
    in_specs = (
        P("batch", "blk", None),
        P("batch", "blk"),
        P("batch"),
        P(),
        P(),
        P(),
        P(),
        P(),
        P(),
        P(),
        P(),
        P(),
        P(),
        P(),
        P(),
        P(),
        P("batch", "blk", None),
    )
    out_specs = (
        P("batch", "blk", None),
        P("batch", "blk", None),
        P(),
        P(),
        P(),
        P(),
        P(),
        P(),
        P(),
        P(),
        P(),
        P(),
        P(),
        P(),
        P(),
        P(),
    )
    return jax.shard_map(body, mesh=mesh, in_specs=in_specs, out_specs=out_specs, check_vma=False)
```

```python
from functools import partial
from types import SimpleNamespace

import jax
import jax.numpy as jnp
from jax import lax
from jax.experimental import pallas as pl
from jax.experimental.pallas import tpu as pltpu
from jax.sharding import PartitionSpec as P

HEAD_DIM = 64


masked_score = -1e30
norm_eps = 1e-05


MESH = pl.DeviceIdType.MESH


def coordinates():
    batch, blk = lax.axis_index("batch"), lax.axis_index("blk")
    return dict(
        core=lax.rem(blk, 2),
        x=lax.div(blk, 2),
        y=lax.rem(batch, 2),
        l=lax.rem(lax.div(batch, 2), 2),
        h=lax.rem(lax.div(batch, 4), 2),
        far=lax.div(batch, 8),
    )


def device_at(place, **changes):
    at = SimpleNamespace(**{**place, **changes})
    return (at.far * 8 + at.h * 4 + at.l * 2 + at.y, at.x * 2 + at.core)


def across(place, d):
    return device_at(place, **{d: 1 - place[d]})


def flipped(index, bit):
    return index + bit - 2 * bit * lax.rem(lax.div(index, bit), 2)


def far_bits(far):
    return [1 << b for b in range(far.bit_length() - 1)]


def far_hops(place, far):
    return [device_at(place, far=flipped(place["far"], bit)) for bit in far_bits(far)]


def greet(place, far):
    partners = [across(place, d) for d in ("core", "x", "y", "l", "h")]
    partners += far_hops(place, far)
    partners.append(device_at(place, x=1 - place["x"], core=1 - place["core"]))
    barrier = pltpu.get_barrier_semaphore()
    for partner in partners:
        pl.semaphore_signal(barrier, inc=1, device_id=partner, device_id_type=MESH)
    pl.semaphore_wait(barrier, len(partners))


class Chunk:
    def __init__(self, matrix, row, row_step, col, col_step, width, order, far):
        self.matrix, self.width, self.order, self.far = matrix, width, order, far
        self.row, self.row_step, self.col, self.col_step = row, row_step, col, col_step
        self.share = 768 >> len(order)
        self.received = 768 - self.share + self.share * len(far_bits(far))
        self.copies = 2 + 2 * len(order) + len(far_bits(far))

    def region(self, ref, half, row, rows):
        row = self.row + half * self.row_step + row
        col = self.col + half * self.col_step
        return ref.at[
            pl.ds(pl.multiple_of(row, 16), rows), pl.ds(pl.multiple_of(col, 128), self.width)
        ]

    def steps(self, place, own, whole, core_box, inbox, send_sems, recv_sems, store_sem):
        sent = []

        def send(source, target, device):
            i = len(sent)
            copy = pltpu.make_async_remote_copy(
                src_ref=source,
                dst_ref=target,
                send_sem=send_sems.at[i],
                recv_sem=recv_sems.at[i],
                device_id=device,
                device_id_type=MESH,
            )
            copy.start()
            sent.append(copy)
            return copy

        def add(row, rows, froms, inbox=inbox):
            tile = min(rows, 48)

            def one(t, carry):
                at = pl.multiple_of(t * tile, 16)
                here = self.region(own, core, row + at, tile)
                total = here[...].astype(jnp.float32)
                for start in froms:
                    total = total + inbox[pl.ds(pl.multiple_of(start + at, 16), tile), :].astype(
                        jnp.float32
                    )
                here[...] = total.astype(jnp.bfloat16)
                return carry

            lax.fori_loop(0, rows // tile, one, 0)

        core = place["core"]
        copy = send(
            self.region(own, 1 - core, 0, 768),
            core_box,
            device_at(place, core=1 - core),
        )
        yield
        copy.wait_recv()
        add(0, 768, (0,), core_box)
        yield
        row, rows, used = 0, 768, 0
        for d in self.order:
            rows //= 2
            copy = send(
                self.region(own, core, row + (1 - place[d]) * rows, rows),
                inbox.at[pl.ds(used, rows)],
                across(place, d),
            )
            row = row + place[d] * rows
            yield
            copy.wait_recv()
            add(row, rows, (used,))
            used += rows
            yield
        for device in far_hops(place, self.far):
            copy = send(self.region(own, core, row, rows), inbox.at[pl.ds(used, rows)], device)
            yield
            copy.wait_recv()
            copy.wait_send()
            sent[-1] = None
            add(row, rows, (used,))
            used += rows
        store = pltpu.make_async_copy(
            self.region(own, core, row, rows), self.region(whole, core, row, rows), store_sem
        )
        store.start()
        source = own
        for d in reversed(self.order):
            copy = send(
                self.region(source, core, row, rows),
                self.region(whole, core, row, rows),
                across(place, d),
            )
            yield
            copy.wait_recv()
            if source is own:
                store.wait()
            source = whole
            row = row - place[d] * rows
            rows *= 2
            yield
        copy = send(
            self.region(whole, core, 0, 768),
            self.region(whole, core, 0, 768),
            device_at(place, core=1 - core),
        )
        yield
        copy.wait_recv()
        yield
        for copy in sent:
            if copy is not None:
                copy.wait_send()


def vector_hops(place, far):
    return [across(place, d) for d in ("core", "x", "y", "l", "h")] + far_hops(place, far)


def vector_steps(place, far, totals, inbox, send_sems, recv_sems):
    sent = []
    for i, device in enumerate(vector_hops(place, far)):
        copy = pltpu.make_async_remote_copy(
            src_ref=totals.at[i],
            dst_ref=inbox.at[i],
            send_sem=send_sems.at[i],
            recv_sem=recv_sems.at[i],
            device_id=device,
            device_id_type=MESH,
        )
        copy.start()
        sent.append(copy)
        yield
        copy.wait_recv()
        totals[i + 1] = totals[i] + inbox[i]
        yield
    for copy in sent:
        copy.wait_send()


LINKS = ("lyxh", "yxlh", "lyhx", "lyhx", "yxlh", "xylh", "lxyh", "ylxh", "xylh", "xylh", "xylh", "yxlh")
PLAN = (
    13, 4, 0, 14, 5, 1, 15, 4, 4, 0, 0, 6, 2, 16, 5, 5, 1, 1, 3, 7, 17, 6, 8, 6, 18, 3, 3, 0,
    0, 2, 19, 4, 4, 8, 8, 7, 7, 5, 2, 20, 21, 5, 22, 23, 1, 1, 24, 25, 4, 4, 0, 26, 9, 0, 27, 6,
    6, 28, 5, 5, 29, 8, 8, 9, 9, 4, 4, 7, 7, 3, 3, 1, 1, 30, 31, 5, 10, 6, 5, 2, 6, 0, 0, 2,
    4, 32, 8, 8, 1, 1, 4, 10, 10, 3, 11, 9, 9, 33, 5, 5, 0, 0, 6, 12, 7, 7, 11, 11, 2, 8, 1, 4,
    4, 8, 6, 12, 12, 9, 9, 5, 5, 1, 0, 0, 3, 4, 4, 7, 8, 8, 6, 11, 11, 12, 12, 9, 10, 10, 1, 1,
    9, 2, 5, 5, 12, 12, 0, 0, 8, 8, 7, 3, 3, 9, 9, 6, 1, 1, 10, 10, 4, 4, 3, 3, 2, 2, 7, 7,
    12, 12, 11, 11, 5, 5, 8, 8, 0, 0, 9, 9, 6, 6, 10, 10, 12, 7, 7, 3, 3, 2, 2, 11, 11, 10, 10, 1,
    1, 9, 9, 6, 6, 2, 2, 7, 7, 8, 8, 11, 11, 4, 4, 3, 3, 10, 10, 4, 11, 11, 2, 2, 5, 5, 9, 9,
    6, 6, 10, 10, 0, 0, 5, 3, 3, 7, 7, 11, 11, 8, 8, 1, 1, 0, 2, 2, 8, 1, 9, 9, 10, 10, 11, 11,
    9, 6, 6, 7, 7, 6, 3, 3, 7, 10, 10, 11, 11, 2, 2, 3, 10, 11, 2,
)


def chunks_of(far):
    parts = [("down", j * 768, 0) for j in range(4)] + [("up", 0, j * 768) for j in range(4)]
    parts += [("out", 0, 0)]
    chunks = [
        Chunk(matrix, row, 0, col, 384, 384, links, far)
        for (matrix, row, col), links in zip(parts, LINKS)
    ]
    for (col, step), links in zip(((0, 768), (1536, 384), (384, 768)), LINKS[9:]):
        chunks.append(Chunk("into", 0, 0, col, step, 384, links, far))
    return chunks


F32, LOW = jnp.float32, jnp.bfloat16
PAIR = 2 * HEAD_DIM
VMEM_LIMIT = 127 << 19


def dot(left, right):
    return lax.dot_general(left, right, (((1,), (0,)), ((), ())), preferred_element_type=F32)


def dot_nt(left, right):
    return lax.dot_general(left, right, (((1,), (1,)), ((), ())), preferred_element_type=F32)


def span(start, size, unit):
    return pl.ds(pl.multiple_of(start, unit), size)


def lanes_of(i, rows):
    lane = lax.broadcasted_iota(jnp.int32, (rows, PAIR), 1)
    return lax.div(lane, HEAD_DIM) == i


def remote(source, target, send_sem, recv_sem, device):
    return pltpu.make_async_remote_copy(
        src_ref=source,
        dst_ref=target,
        send_sem=send_sem,
        recv_sem=recv_sem,
        device_id=device,
        device_id_type=MESH,
    )


def here_of(x, cols):
    return span(x * cols, cols, 256)


def count_hops(place, far):
    return [across(place, d) for d in ("y", "l", "h")] + far_hops(place, far)


def layer_kernel(far, names, *refs):
    r = SimpleNamespace(**dict(zip(names, refs)))
    extra = refs[len(names) :]
    r.boxes, r.core_boxes = extra[: len(extra) - 10], extra[len(extra) - 10 :]
    place = coordinates()
    x, core = place["x"], place["core"]
    half, width = r.row_tokens.shape
    cols = half // 2
    ff = r.hidden.shape[1]
    tile = 256
    chunks = chunks_of(far)
    n = len(chunks)
    boxes = [r.boxes[i] for i in range(n)]
    core_boxes = [r.core_boxes[i] for i in range(9)]
    core_boxes += [
        r.down_weight.at[pl.ds(3 * width, width), pl.ds(i * 384, 384)] for i in range(2)
    ]
    core_boxes.append(r.core_boxes[9])
    own = dict(down=r.down_own, up=r.up_own, out=r.up_weight.at[:, pl.ds(3 * width, width)], into=r.up_weight)
    whole = dict(down=r.down_whole, up=r.up_whole, out=r.out_whole, into=r.into_whole)
    other_x = device_at(place, x=1 - x)
    other_core = device_at(place, core=1 - core)
    here, there = here_of(x, cols), here_of(1 - x, cols)
    row_tokens, row_cot = r.row_tokens, r.row_cot
    query, keys, values, bias = r.query, r.keys, r.values, r.bias
    attended, log_total = r.attended, r.log_total
    in_first, in_later = r.down_own, r.down_weight
    out_weight, up_weight, down_weight = r.out_weight, r.up_weight, r.down_weight

    def local(source, target, sem):
        copy = pltpu.make_async_copy(source, target, sem)
        copy.start()
        return copy

    def load_in(target, sems):
        return [
            local(
                r.into_any.at[:, pl.ds(j * width, width)],
                target.at[pl.ds(j * width, width), :],
                sems.at[j],
            )
            for j in range(3)
        ]

    stay_tokens = local(r.tokens_any.at[x], row_tokens.at[here], r.stay_sems.at[0])
    in_loads = load_in(in_first, r.in_sems)
    stay_cot = local(r.cot_any.at[x], row_cot.at[here], r.stay_sems.at[1])
    weight_loads = [
        local(a, b, r.load_sems.at[i])
        for i, (a, b) in enumerate(
            (
                (r.out_any, r.out_weight),
                (r.up_any, r.up_weight),
                (r.down_any, r.down_weight),
            )
        )
    ]
    greet(place, far)
    row_send, row_recv = r.row_send, r.row_recv
    move_tokens = remote(
        r.tokens_any.at[1 - x], row_tokens.at[here], row_send.at[0], row_recv.at[0], other_x
    )
    move_tokens.start()
    ids_out, ids_in = r.ids_out, r.ids_in
    for i in range(2):
        ids_out[i] = jnp.broadcast_to(r.segments[i : i + 1, :], (8, cols))
    blk = x * 2 + core
    moves = []
    for i, (dx, dc) in enumerate(((0, 1), (1, 0), (1, 1))):
        to_x = x + dx - 2 * dx * x
        to_core = core + dc - 2 * dc * core
        moves.append(
            remote(
                ids_out.at[to_x],
                ids_in.at[blk],
                r.id_send.at[i],
                r.id_recv.at[i],
                device_at(place, x=to_x, core=to_core),
            )
        )
        moves[-1].start()
    ids_in[blk] = ids_out[x]
    counts, count_in, keep = r.counts, r.count_in, r.keep
    counts[0] = jnp.full((8, 128), (keep[0] + keep[1]).astype(F32), F32)
    hops = count_hops(place, far)
    count_moves = []

    def hop(i):
        if i:
            count_moves[-1].wait_recv()
            counts[i] = counts[i - 1] + count_in[i - 1]
        if i < len(hops):
            move = remote(
                counts.at[i], count_in.at[i], r.count_send.at[i], r.count_recv.at[i], hops[i]
            )
            move.start()
            count_moves.append(move)

    hop(0)
    move_cot = remote(
        r.cot_any.at[1 - x], row_cot.at[here], row_send.at[1], row_recv.at[1], other_x
    )

    def as_row(ref, part=slice(None)):
        return ref[part].astype(F32).reshape(1, -1)

    def project(rows, at):
        block = row_tokens[rows, :]
        place_rows = span(core * half + at, cols, 256)
        keys[place_rows, :] = dot(block, in_first[width : 2 * width, :]).astype(LOW)
        values[place_rows, :] = (
            dot(block, in_first[2 * width : 3 * width, :]) + as_row(r.value_bias)
        ).astype(LOW)
        return place_rows

    def project_query(rows):
        block = row_tokens[rows, :]
        query[rows, :] = (dot(block, in_first[:width, :]) + as_row(r.query_bias)).astype(
            LOW
        ) * jnp.asarray(HEAD_DIM**-0.5, LOW)

    shares = []
    stay_tokens.wait()
    for load in in_loads:
        load.wait()
    for step, (rows, at) in enumerate(((here, x * cols), (there, (1 - x) * cols))):
        if step == 1:
            move_tokens.wait_recv()
            move_cot.start()
        place_rows = project(rows, at)
        for i, array in enumerate((keys, values)):
            k = step * 2 + i
            move = remote(
                array.at[place_rows],
                array.at[place_rows],
                r.share_send.at[k],
                r.share_recv.at[k],
                other_core,
            )
            move.start()
            shares.append(move)
        project_query(rows)
        hop(1 + step)
    for move in moves:
        move.wait_recv()
    all_ids = jnp.concatenate([ids_in[0], ids_in[2], ids_in[1], ids_in[3]], axis=1).astype(F32)
    column = jnp.broadcast_to(all_ids[0:1, :], (128, 2 * half)).T[:, 0:1]
    own_ids = jnp.concatenate([ids_in[core], ids_in[2 + core]], axis=1).astype(F32)[0:1, :]
    bias[...] = jnp.where(column == own_ids, 0.0, masked_score).astype(LOW)
    for i in range(3, len(hops) + 1):
        hop(i)
    factor = keep[x].astype(F32) * (float(2 * 8 * far) / counts[len(hops)])[0:1, 0:1]
    r.kept[...] = counts[len(hops)].astype(jnp.int32)
    for move in shares:
        move.wait_recv()

    def attend(p, carry):
        pair = span(p * PAIR, PAIR, PAIR)
        values_t = values[:, pair].T
        key_pair = keys[:, pair]
        query_pair = query[:, pair]
        scores = []
        for i in range(2):
            chosen = jnp.where(lanes_of(i, half), query_pair, jnp.zeros_like(query_pair))
            scores.append(dot_nt(key_pair, chosen) + bias[...].astype(F32))
        for i in range(2):
            top = jnp.max(scores[i], axis=0, keepdims=True)
            powered = jnp.exp(scores[i] - top)
            total = jnp.sum(powered, axis=0, keepdims=True)
            mixture = dot(values_t[i * HEAD_DIM : (i + 1) * HEAD_DIM, :], powered.astype(LOW))
            attended[span(p * PAIR + i * HEAD_DIM, HEAD_DIM, HEAD_DIM), :] = mixture / total
            log_total[pl.ds(p * 2 + i, 1), :] = top + jnp.log(total)
        return carry

    lax.fori_loop(0, width // PAIR, attend, 0)

    low, work, normed = r.low, r.work, r.normed
    inverse, first, first_low, first_t = r.inverse, r.first, r.first_low, r.first_t
    hidden, slope, vectors = r.hidden, r.slope, r.vec_totals.at[0]
    second_in, ffn_grad, attended_grad = first, first_low, low
    low[...] = attended[...].T.astype(LOW)
    weight_loads[0].wait()
    work[...] = dot(low[...], out_weight[...])
    mean = partial(jnp.mean, axis=-1, keepdims=True)

    def tiles(step, carry):
        def one(t, kept):
            return step(span(t * tile, tile, tile), kept)

        return lax.fori_loop(0, half // tile, one, carry)

    def normalize(given):
        centered = given - mean(given)
        inv = lax.rsqrt(mean(centered * centered) + norm_eps)
        return centered * inv, inv

    def total_of(given):
        return jnp.sum(given, axis=0, keepdims=True)

    def first_norm(at, carry):
        branch = work[at, :] + as_row(r.out_bias)
        unit, inv = normalize(row_tokens[at, :].astype(F32) + factor * branch)
        normed[at, :] = unit
        inverse[at, :] = jnp.broadcast_to(inv, (tile, 128))
        out = unit * as_row(r.first_gain) + as_row(r.first_shift)
        first[at, :] = out
        first_low[at, :] = out.astype(LOW)
        return carry

    tiles(first_norm, 0)
    first_t[...] = first_low[...].T
    weight_loads[1].wait()

    def up_step(f, carry):
        at = span(f * 512, 512, 512)
        pre = dot(first_low[...], up_weight[:, at]) + as_row(r.up_bias, at)
        chance = 0.5 + 0.5 * lax.erf(pre * (2.0**-0.5))
        density = jnp.exp(pre * pre * -0.5) * 0.3989422804014327
        hidden[:, at] = (pre * chance).astype(LOW)
        slope[:, at] = (chance + pre * density).astype(LOW)
        return carry

    lax.fori_loop(0, ff // 512, up_step, 0)
    weight_loads[2].wait()
    work[...] = dot(hidden[...], down_weight[...])
    zero = jnp.zeros((1, width), F32)
    move_cot.wait_recv()
    stay_cot.wait()

    def second_norm(at, carry):
        gain_sum, shift_sum, bias_sum = carry
        gain = as_row(r.second_gain)
        unit, inv = normalize(first[at, :] + factor * (work[at, :] + as_row(r.down_bias)))
        grad = row_cot[at, :].astype(F32)
        row_cot[at, :] = (unit * gain + as_row(r.second_shift)).astype(LOW)
        scaled = grad * gain
        inner = inv * (scaled - mean(scaled) - unit * mean(scaled * unit))
        second_in[at, :] = inner
        low_grad = (factor * inner).astype(LOW)
        ffn_grad[at, :] = low_grad
        return (
            gain_sum + total_of(grad * unit),
            shift_sum + total_of(grad),
            bias_sum + total_of(low_grad.astype(F32)),
        )

    second_gain_sum, second_shift_sum, down_sum = tiles(second_norm, (zero, zero, zero))
    vectors[...] = jnp.zeros_like(vectors)
    vectors[5:6, :] = down_sum
    vectors[6:7, :] = second_gain_sum
    vectors[7:8, :] = second_shift_sum
    mixed, tokens_grad = r.mixed, r.tokens_grad
    move_mixed = remote(row_cot.at[there], mixed.at[x], row_send.at[2], row_recv.at[2], other_x)
    move_mixed.start()
    stay_mixed = local(row_cot.at[here], mixed.at[x], r.stay_sems.at[2])

    offsets = [sum(c.copies for c in chunks[:i]) for i in range(n)]
    gens = {}

    def advance(i):
        if i == n and i not in gens:
            gens[i] = vector_steps(place, far, r.vec_totals, r.vec_inbox, r.vec_send, r.vec_recv)
        if i not in gens:
            part = pl.ds(offsets[i], chunks[i].copies)
            gens[i] = chunks[i].steps(
                place,
                own[chunks[i].matrix],
                whole[chunks[i].matrix],
                core_boxes[i],
                boxes[i],
                r.send_sems.at[part],
                r.recv_sems.at[part],
                r.store_sems.at[i],
            )
        next(gens[i], None)

    def feed_back(f):
        at = pl.ds(f * width, width)
        pulled = dot_nt(ffn_grad[...], down_weight[at, :])
        pre_grad = (slope[:, at].astype(F32) * pulled).astype(LOW)
        slope[:, at] = pre_grad
        own["down"][at, :] = dot(hidden[:, at].T, ffn_grad[...]).astype(LOW)
        own["up"][:, at] = dot(first_t[...], pre_grad).astype(LOW)
        part = dot_nt(pre_grad, up_weight[:, at])
        if f:
            work[...] += part
        else:
            work[...] = part
        vectors[8 + f : 9 + f, :] = total_of(pre_grad.astype(F32))

    tokens_t, delta = first_t, r.delta
    in_again = []

    def first_back(at, carry):
        gain_sum, shift_sum, bias_sum = carry
        grad = second_in[at, :] + work[at, :]
        unit = normed[at, :]
        scaled = grad * as_row(r.first_gain)
        inner = inverse[at, 0:1] * (scaled - mean(scaled) - unit * mean(scaled * unit))
        work[at, :] = inner
        low_grad = (factor * inner).astype(LOW)
        ffn_grad[at, :] = low_grad
        return (
            gain_sum + total_of(grad * unit),
            shift_sum + total_of(grad),
            bias_sum + total_of(low_grad.astype(F32)),
        )

    def norm_back():
        in_again.extend(load_in(in_later, r.in_sems))
        first_gain_sum, first_shift_sum, out_sum = tiles(first_back, (zero, zero, zero))
        vectors[2:3, :] = out_sum
        vectors[3:4, :] = first_gain_sum
        vectors[4:5, :] = first_shift_sum
        branch_grad = ffn_grad[...]
        own["out"][...] = dot(attended[...].astype(LOW), branch_grad).astype(LOW)
        attended_grad[...] = dot_nt(branch_grad, out_weight[...]).astype(LOW)
        product = dot_nt(out_weight[...], branch_grad).astype(LOW).astype(F32) * attended[...]
        delta[...] = jnp.zeros_like(delta)
        for h in range(width // HEAD_DIM):
            delta[h : h + 1, :] = total_of(product[h * HEAD_DIM : (h + 1) * HEAD_DIM, :])
        tokens_t[...] = row_tokens[...].T

    query_t, joined, other, arrived = attended, hidden, slope, r.arrived
    mine = (normed, first)
    pair_moves = []

    def one_side(p, side, fresh):
        pair = pl.ds(p * PAIR, PAIR)
        at = span(side * half, half, 512)
        key_pair, value_pair = keys[at, pair], values[at, pair]
        keys_t = key_pair.T
        query_pair, grad_pair = query[:, pair], attended_grad[:, pair]
        none = jnp.zeros_like(query_pair)
        heads = [pl.ds(p * 2 + i, 1) for i in range(2)]
        chosen = [jnp.where(lanes_of(i, half), query_pair, none) for i in range(2)]
        pulled = [jnp.where(lanes_of(i, half), grad_pair, none) for i in range(2)]
        mask = bias[at, :].astype(F32)
        scores = [dot_nt(key_pair, chosen[i]) + mask for i in range(2)]
        pull = [dot_nt(value_pair, pulled[i]) - delta[heads[i], :] for i in range(2)]
        chance = [jnp.exp(scores[i] - log_total[heads[i], :]) for i in range(2)]
        score_grad = [(chance[i] * pull[i]).astype(LOW) for i in range(2)]
        value_sum = sum(dot(chance[i].astype(LOW), pulled[i]) for i in range(2))
        key_sum = sum(dot(score_grad[i], chosen[i]) for i in range(2))
        for i in range(2):
            lines = pl.ds(p * PAIR + i * HEAD_DIM, HEAD_DIM)
            query_part = dot(keys_t[i * HEAD_DIM : (i + 1) * HEAD_DIM, :], score_grad[i])
            if fresh:
                query_t[lines, :] = query_part
            else:
                query_t[lines, :] += query_part
        return key_sum, value_sum

    def attend_back(p, mine_too):
        pair = pl.ds(p * PAIR, PAIR)
        if mine_too:
            key_sum, value_sum = one_side(p, core, False)
            mine[0][:, pair] = key_sum
            mine[1][:, pair] = value_sum
            return
        for i, part in enumerate(one_side(p, 1 - core, True)):
            at = pl.ds(i * width + p * PAIR, PAIR)
            other[:, at] = part.astype(LOW)
            k = p * 2 + i
            move = remote(
                other.at[:, at],
                arrived.at[:, at],
                r.pair_send.at[k],
                r.pair_recv.at[k],
                other_core,
            )
            move.start()
            pair_moves.append(move)

    def join(j, at):
        to = pl.ds(j * width + at.start, at.size)
        if j == 0:
            joined[:, to] = (query_t[at, :].T * HEAD_DIM**-0.5).astype(LOW)
        else:
            sent = pl.ds((j - 1) * width + at.start, at.size)
            joined[:, to] = (mine[j - 1][:, at] + arrived[:, sent].astype(F32)).astype(LOW)
        own["into"][:, to] = dot(tokens_t[...], joined[:, to]).astype(LOW)

    def wait_pairs(start, stop):
        for move in pair_moves[2 * start : 2 * stop]:
            move.wait_recv()

    some, rest, every = pl.ds(0, width // 2), pl.ds(width // 2, width // 2), pl.ds(0, width)
    pairs = width // PAIR

    def join_some():
        wait_pairs(0, pairs // 2)
        join(0, some)
        join(1, some)

    def join_values():
        wait_pairs(pairs // 2, pairs)
        join(2, every)

    def join_rest():
        join(0, rest)
        join(1, rest)
        for i, j in ((0, 0), (1, 2)):
            vectors[i : i + 1, :] = total_of(joined[:, j * width : (j + 1) * width].astype(F32))

    row_grad = slope.at[:, pl.ds(2 * width, width)]
    last_moves = []

    def finish_rows():
        for load in in_again:
            load.wait()
        total = work[...]
        for j in range(3):
            at = pl.ds(j * width, width)
            total = total + dot_nt(joined[:, at], in_later[at, :])
        row_grad[...] = total.astype(LOW)
        last_moves.append(
            remote(row_grad.at[there], tokens_grad.at[x], row_send.at[3], row_recv.at[3], other_x)
        )
        last_moves[0].start()
        last_moves.append(local(row_grad.at[here], tokens_grad.at[x], r.stay_sems.at[3]))

    halves = [partial(attend_back, p, side) for p in range(pairs) for side in (False, True)]
    pieces = [partial(feed_back, f) for f in range(ff // width)] + [norm_back]
    pieces += [*halves[:8], join_some, *halves[8:], join_values, join_rest, finish_rows]
    for turn in PLAN:
        if turn <= n:
            advance(turn)
        else:
            pieces[turn - n - 1]()
    for i in range(n + 1):
        for _ in gens[i]:
            pass
    r.vector_out[...] = r.vec_totals[len(vector_hops(place, far))]
    stay_mixed.wait()
    move_mixed.wait()
    for move in last_moves:
        move.wait()
    for move in [move_tokens, move_cot, *moves, *count_moves, *shares, *pair_moves]:
        move.wait_send()


def layer(tokens, cot, segments, keep, weights, vectors, far):
    _, cols, width = tokens.shape
    half = 2 * cols
    ff = weights[2].shape[1]
    chunks = chunks_of(far)
    hops = 5 + len(far_bits(far))
    counts = 3 + len(far_bits(far))
    copies = sum(c.copies for c in chunks)
    vmem, any_space = pl.BlockSpec(memory_space=pltpu.VMEM), pl.BlockSpec(memory_space=pl.ANY)
    smem = pl.BlockSpec(memory_space=pltpu.SMEM)
    shape = jax.ShapeDtypeStruct

    def dma(count):
        return pltpu.SemaphoreType.DMA((count,))

    inputs = dict(
        tokens_any=(tokens, any_space),
        cot_any=(cot, any_space),
        segments=(segments, vmem),
        keep=(keep, smem),
        into_any=(weights[0], any_space),
        out_any=(weights[1], any_space),
        up_any=(weights[2], any_space),
        down_any=(weights[3], any_space),
        **{k: (v, vmem) for k, v in vectors.items()},
    )
    outputs = dict(
        into_whole=(shape((width, 3 * width), LOW), any_space),
        out_whole=(shape((width, width), LOW), any_space),
        up_whole=(shape((width, ff), LOW), any_space),
        down_whole=(shape((ff, width), LOW), any_space),
        vector_out=(shape((16, width), F32), vmem),
        mixed=(shape(tokens.shape, LOW), any_space),
        tokens_grad=(shape(tokens.shape, LOW), any_space),
        kept=(shape((8, 128), jnp.int32), vmem),
    )
    scratch = dict(
        out_weight=((width, width), LOW),
        up_weight=((width, ff), LOW),
        down_weight=((ff, width), LOW),
        up_own=((width, ff), LOW),
        down_own=((ff, width), LOW),
        row_tokens=((half, width), LOW),
        row_cot=((half, width), LOW),
        query=((half, width), LOW),
        keys=((2 * half, width), LOW),
        values=((2 * half, width), LOW),
        bias=((2 * half, half), LOW),
        attended=((width, half), F32),
        log_total=((16, half), F32),
        delta=((16, half), F32),
        low=((half, width), LOW),
        work=((half, width), F32),
        normed=((half, width), F32),
        inverse=((half, 128), F32),
        first=((half, width), F32),
        first_low=((half, width), LOW),
        first_t=((width, half), LOW),
        hidden=((half, ff), LOW),
        slope=((half, ff), LOW),
        arrived=((half, 2 * width), LOW),
        ids_out=((2, 8, cols), jnp.int32),
        ids_in=((4, 8, cols), jnp.int32),
        counts=((counts + 1, 8, 128), F32),
        count_in=((counts, 8, 128), F32),
        vec_inbox=((hops, 16, width), F32),
        vec_totals=((hops + 1, 16, width), F32),
    )
    sems = dict(
        in_sems=3,
        load_sems=3,
        stay_sems=4,
        row_send=4,
        row_recv=4,
        id_send=3,
        id_recv=3,
        count_send=counts,
        count_recv=counts,
        share_send=4,
        share_recv=4,
        pair_send=2 * width // PAIR,
        pair_recv=2 * width // PAIR,
        send_sems=copies,
        recv_sems=copies,
        store_sems=len(chunks),
        vec_send=hops,
        vec_recv=hops,
    )
    boxes = [((c.received, c.width), LOW) for c in chunks]
    boxes += [((width, c.width), LOW) for c in chunks[:10]]
    names = [*inputs, *outputs, *scratch, *sems]
    return pl.pallas_call(
        partial(layer_kernel, far, names),
        out_shape=[o[0] for o in outputs.values()],
        in_specs=[i[1] for i in inputs.values()],
        out_specs=[o[1] for o in outputs.values()],
        scratch_shapes=[pltpu.VMEM(a, t) for a, t in scratch.values()]
        + [dma(c) for c in sems.values()]
        + [pltpu.VMEM(a, t) for a, t in boxes],
        compiler_params=pltpu.CompilerParams(
            collective_id=0, has_side_effects=True, vmem_limit_bytes=VMEM_LIMIT
        ),
        name="layer",
    )(*[i[0] for i in inputs.values()])


def finish_kernel(*refs):
    given, (vectors, kept, mixed, tokens_grad), outs = refs[:4], refs[4:8], refs[8:12]
    (query_b, value_b, out_b, first_g, first_s, up_b, down_b, second_g, second_s) = refs[12:21]
    kept_out, mixed_out, tokens_out = refs[21:24]
    low, wide, load_sems, store_sems, row_sems = refs[24:28], refs[28:32], *refs[32:35]
    held = refs[35:37]
    rows_in = [
        pltpu.make_async_copy(a, b, row_sems.at[i])
        for i, (a, b) in enumerate(zip((mixed, tokens_grad), held))
    ]
    rows_out = [
        pltpu.make_async_copy(a, b, row_sems.at[2 + i])
        for i, (a, b) in enumerate(zip(held, (mixed_out, tokens_out)))
    ]
    tiles = []
    for m, ref in enumerate(given):
        height = 196608 // ref.shape[1] // 16 * 16
        height = next(h for h in range(height, 0, -16) if ref.shape[0] % h == 0)
        tiles += [(m, pl.ds(at, height)) for at in range(0, ref.shape[0], height)]
    loads = [
        pltpu.make_async_copy(given[m].at[at], low[m].at[at], load_sems.at[i])
        for i, (m, at) in enumerate(tiles)
    ]
    stores = [
        pltpu.make_async_copy(wide[m].at[at], outs[m].at[at], store_sems.at[i])
        for i, (m, at) in enumerate(tiles)
    ]
    for load in loads:
        load.start()
    for row in rows_in:
        row.start()
    small = (query_b, value_b, out_b, first_g, first_s, down_b, second_g, second_s)
    kept_out[...] = kept[0:1, 0:1].reshape((1,))
    for i, ref in enumerate(small):
        ref[...] = vectors[i : i + 1, :].reshape(ref.shape)
    width = vectors.shape[1]
    for i in range(up_b.shape[0] // width):
        up_b[pl.ds(i * width, width)] = vectors[8 + i : 9 + i, :].reshape((width,))
    for load, store, (m, at) in zip(loads, stores, tiles):
        load.wait()
        piece = 32 if at.size % 32 == 0 else 16

        def convert(t, carry):
            part = span(at.start + t * piece, piece, 16)
            wide[m][part, :] = low[m][part, :].astype(F32)
            return carry

        lax.fori_loop(0, at.size // piece, convert, 0)
        store.start()
    for row_in, row_out in zip(rows_in, rows_out):
        row_in.wait()
        row_out.start()
    for copy in [*stores, *rows_out]:
        copy.wait()


def finish(matrices, vectors, kept, mixed, tokens_grad):
    width = vectors.shape[1]
    ff = matrices[2].shape[1]
    vmem, any_space = pl.BlockSpec(memory_space=pltpu.VMEM), pl.BlockSpec(memory_space=pl.ANY)
    shape = jax.ShapeDtypeStruct
    sizes = [width, width, width, width, width, ff, width, width, width]
    return pl.pallas_call(
        finish_kernel,
        out_shape=[shape(m.shape, F32) for m in matrices]
        + [shape((k,), F32) for k in sizes]
        + [shape((1,), jnp.int32), shape(mixed.shape, LOW), shape(tokens_grad.shape, LOW)],
        in_specs=[any_space] * 4 + [vmem] * 2 + [any_space] * 2,
        out_specs=[any_space] * 4 + [vmem] * 10 + [any_space] * 2,
        scratch_shapes=[pltpu.VMEM(m.shape, LOW) for m in matrices]
        + [pltpu.VMEM(m.shape, F32) for m in matrices]
        + [
            pltpu.SemaphoreType.DMA((64,)),
            pltpu.SemaphoreType.DMA((64,)),
            pltpu.SemaphoreType.DMA((4,)),
            pltpu.VMEM(mixed.shape, LOW),
            pltpu.VMEM(tokens_grad.shape, LOW),
        ],
        compiler_params=pltpu.CompilerParams(vmem_limit_bytes=VMEM_LIMIT),
        name="finish",
    )(*matrices, vectors, kept, mixed, tokens_grad)


def body(
    tokens,
    segment_ids,
    keep_flags,
    input_weight,
    query_bias,
    value_bias,
    output_weight,
    output_bias,
    first_gain,
    first_shift,
    up_weight,
    up_bias,
    down_weight,
    down_bias,
    second_gain,
    second_shift,
    cotangent,
):
    far = lax.axis_size("batch") // 8
    *low, vectors, mixed, tokens_grad, kept = layer(
        tokens,
        cotangent,
        segment_ids,
        keep_flags,
        (input_weight, output_weight, up_weight, down_weight),
        dict(
            query_bias=query_bias,
            value_bias=value_bias,
            out_bias=output_bias,
            first_gain=first_gain,
            first_shift=first_shift,
            up_bias=up_bias,
            down_bias=down_bias,
            second_gain=second_gain,
            second_shift=second_shift,
        ),
        far,
    )
    into, out, up, down, *small, kept, mixed, tokens_grad = finish(
        low, vectors, kept, mixed, tokens_grad
    )
    query_b, value_b, out_b, first_g, first_s, up_b, down_b, second_g, second_s = small
    return (
        mixed,
        tokens_grad,
        kept.reshape(()),
        into,
        query_b,
        value_b,
        out,
        out_b,
        first_g,
        first_s,
        up,
        up_b,
        down,
        down_b,
        second_g,
        second_s,
    )


def solution(mesh):
    in_specs = (
        P("batch", "blk", None),
        P("batch", "blk"),
        P("batch"),
        P(),
        P(),
        P(),
        P(),
        P(),
        P(),
        P(),
        P(),
        P(),
        P(),
        P(),
        P(),
        P(),
        P("batch", "blk", None),
    )
    out_specs = (
        P("batch", "blk", None),
        P("batch", "blk", None),
        P(),
        P(),
        P(),
        P(),
        P(),
        P(),
        P(),
        P(),
        P(),
        P(),
        P(),
        P(),
        P(),
        P(),
    )
    return jax.shard_map(body, mesh=mesh, in_specs=in_specs, out_specs=out_specs, check_vma=False)
```

```python
from functools import partial
from types import SimpleNamespace

import jax
import jax.numpy as jnp
from jax import lax
from jax.experimental import pallas as pl
from jax.experimental.pallas import tpu as pltpu
from jax.sharding import PartitionSpec as P

HEAD_DIM = 64


masked_score = -1e30
norm_eps = 1e-05


MESH = pl.DeviceIdType.MESH


def coordinates():
    batch, blk = lax.axis_index("batch"), lax.axis_index("blk")
    return dict(
        core=lax.rem(blk, 2),
        x=lax.div(blk, 2),
        y=lax.rem(batch, 2),
        l=lax.rem(lax.div(batch, 2), 2),
        h=lax.rem(lax.div(batch, 4), 2),
        far=lax.div(batch, 8),
    )


def device_at(place, **changes):
    at = SimpleNamespace(**{**place, **changes})
    return (at.far * 8 + at.h * 4 + at.l * 2 + at.y, at.x * 2 + at.core)


def across(place, d):
    return device_at(place, **{d: 1 - place[d]})


def flipped(index, bit):
    return index + bit - 2 * bit * lax.rem(lax.div(index, bit), 2)


def far_bits(far):
    return [1 << b for b in range(far.bit_length() - 1)]


def far_hops(place, far):
    return [device_at(place, far=flipped(place["far"], bit)) for bit in far_bits(far)]


def greet(place, far):
    partners = [across(place, d) for d in ("core", "x", "y", "l", "h")]
    partners += far_hops(place, far)
    partners.append(device_at(place, x=1 - place["x"], core=1 - place["core"]))
    barrier = pltpu.get_barrier_semaphore()
    for partner in partners:
        pl.semaphore_signal(barrier, inc=1, device_id=partner, device_id_type=MESH)
    pl.semaphore_wait(barrier, len(partners))


class Chunk:
    def __init__(self, matrix, row, row_step, col, col_step, width, order, far):
        self.matrix, self.width, self.order, self.far = matrix, width, order, far
        self.row, self.row_step, self.col, self.col_step = row, row_step, col, col_step
        self.share = 768 >> len(order)
        self.received = 768 - self.share + self.share * len(far_bits(far))
        self.copies = 2 + 2 * len(order) + len(far_bits(far))

    def region(self, ref, half, row, rows):
        row = self.row + half * self.row_step + row
        col = self.col + half * self.col_step
        return ref.at[
            pl.ds(pl.multiple_of(row, 16), rows), pl.ds(pl.multiple_of(col, 128), self.width)
        ]

    def steps(self, place, own, whole, core_box, inbox, send_sems, recv_sems, store_sem):
        sent = []

        def send(source, target, device):
            i = len(sent)
            copy = pltpu.make_async_remote_copy(
                src_ref=source,
                dst_ref=target,
                send_sem=send_sems.at[i],
                recv_sem=recv_sems.at[i],
                device_id=device,
                device_id_type=MESH,
            )
            copy.start()
            sent.append(copy)
            return copy

        def add(row, rows, froms, inbox=inbox):
            tile = min(rows, 96)

            def one(t, carry):
                at = pl.multiple_of(t * tile, 16)
                here = self.region(own, core, row + at, tile)
                total = here[...]
                for start in froms:
                    total = total + inbox[pl.ds(pl.multiple_of(start + at, 16), tile), :]
                here[...] = total
                return carry

            lax.fori_loop(0, rows // tile, one, 0)

        core = place["core"]
        copy = send(
            self.region(own, 1 - core, 0, 768),
            core_box,
            device_at(place, core=1 - core),
        )
        yield
        copy.wait_recv()
        add(0, 768, (0,), core_box)
        yield
        row, rows, used = 0, 768, 0
        for d in self.order:
            rows //= 2
            copy = send(
                self.region(own, core, row + (1 - place[d]) * rows, rows),
                inbox.at[pl.ds(used, rows)],
                across(place, d),
            )
            row = row + place[d] * rows
            yield
            copy.wait_recv()
            add(row, rows, (used,))
            used += rows
            yield
        for device in far_hops(place, self.far):
            copy = send(self.region(own, core, row, rows), inbox.at[pl.ds(used, rows)], device)
            yield
            copy.wait_recv()
            copy.wait_send()
            sent[-1] = None
            add(row, rows, (used,))
            used += rows
        store = pltpu.make_async_copy(
            self.region(own, core, row, rows), self.region(whole, core, row, rows), store_sem
        )
        store.start()
        source = own
        for d in reversed(self.order):
            copy = send(
                self.region(source, core, row, rows),
                self.region(whole, core, row, rows),
                across(place, d),
            )
            yield
            copy.wait_recv()
            if source is own:
                store.wait()
            source = whole
            row = row - place[d] * rows
            rows *= 2
            yield
        copy = send(
            self.region(whole, core, 0, 768),
            self.region(whole, core, 0, 768),
            device_at(place, core=1 - core),
        )
        yield
        copy.wait_recv()
        yield
        for copy in sent:
            if copy is not None:
                copy.wait_send()


def vector_hops(place, far):
    return [across(place, d) for d in ("core", "x", "y", "l", "h")] + far_hops(place, far)


def vector_steps(place, far, totals, inbox, send_sems, recv_sems):
    sent = []
    for i, device in enumerate(vector_hops(place, far)):
        copy = pltpu.make_async_remote_copy(
            src_ref=totals.at[i],
            dst_ref=inbox.at[i],
            send_sem=send_sems.at[i],
            recv_sem=recv_sems.at[i],
            device_id=device,
            device_id_type=MESH,
        )
        copy.start()
        sent.append(copy)
        yield
        copy.wait_recv()
        totals[i + 1] = totals[i] + inbox[i]
        yield
    for copy in sent:
        copy.wait_send()


LINKS = ("lxyh", "yxlh", "xylh", "yxlh", "xlhy", "lyhx", "xylh", "yxlh", "lyxh", "lyxh", "xylh", "yxlh")
PLAN = (
    13, 0, 14, 1, 15, 2, 16, 3, 17, 0, 4, 0, 1, 1, 18, 3, 5, 2, 3, 2, 4, 4, 19, 6, 20, 5, 7, 5,
    21, 6, 8, 0, 7, 7, 1, 22, 23, 1, 3, 8, 8, 3, 24, 5, 5, 25, 4, 4, 2, 26, 2, 27, 0, 6, 28, 7,
    29, 1, 1, 3, 3, 30, 5, 5, 9, 31, 4, 4, 8, 8, 2, 2, 7, 32, 33, 1, 1, 3, 0, 3, 9, 0, 34, 9,
    35, 8, 10, 5, 8, 2, 5, 7, 7, 0, 2, 6, 6, 0, 36, 4, 4, 3, 3, 10, 10, 1, 1, 12, 11, 37, 8, 8,
    12, 12, 4, 4, 5, 2, 2, 6, 6, 11, 11, 0, 7, 3, 0, 1, 1, 5, 7, 4, 9, 9, 4, 8, 12, 8, 2, 2,
    0, 3, 5, 6, 12, 5, 7, 10, 10, 1, 1, 0, 7, 11, 11, 8, 6, 9, 12, 12, 4, 4, 2, 2, 3, 0, 9, 7,
    7, 10, 10, 8, 5, 5, 12, 12, 6, 6, 1, 1, 3, 2, 11, 11, 2, 4, 9, 9, 12, 6, 6, 8, 8, 7, 10, 10,
    5, 5, 4, 11, 11, 9, 9, 6, 3, 10, 10, 3, 6, 11, 11, 9, 8, 8, 9, 1, 1, 10, 10, 2, 2, 7, 11, 11,
    1, 0, 9, 9, 6, 2, 4, 4, 6, 10, 10, 3, 3, 5, 5, 11, 11, 4, 7, 7, 9, 9, 0, 0, 3, 5, 8, 8,
    10, 10, 8, 11, 11, 7, 7, 6, 6, 7, 9, 9, 0, 0, 6, 10, 10, 11, 11, 9, 0, 10, 11,
)


def chunks_of(far):
    parts = [("down", j * 768, 0) for j in range(4)] + [("up", 0, j * 768) for j in range(4)]
    parts += [("out", 0, 0)]
    chunks = [
        Chunk(matrix, row, 0, col, 384, 384, links, far)
        for (matrix, row, col), links in zip(parts, LINKS)
    ]
    for (col, step), links in zip(((0, 768), (1536, 384), (384, 768)), LINKS[9:]):
        chunks.append(Chunk("into", 0, 0, col, step, 384, links, far))
    return chunks


F32, LOW = jnp.float32, jnp.bfloat16
PAIR = 2 * HEAD_DIM
VMEM_LIMIT = 127 << 19


def dot(left, right):
    return lax.dot_general(left, right, (((1,), (0,)), ((), ())), preferred_element_type=F32)


def dot_nt(left, right):
    return lax.dot_general(left, right, (((1,), (1,)), ((), ())), preferred_element_type=F32)


def span(start, size, unit):
    return pl.ds(pl.multiple_of(start, unit), size)


def lanes_of(i, rows):
    lane = lax.broadcasted_iota(jnp.int32, (rows, PAIR), 1)
    return lax.div(lane, HEAD_DIM) == i


def remote(source, target, send_sem, recv_sem, device):
    return pltpu.make_async_remote_copy(
        src_ref=source,
        dst_ref=target,
        send_sem=send_sem,
        recv_sem=recv_sem,
        device_id=device,
        device_id_type=MESH,
    )


def here_of(x, cols):
    return span(x * cols, cols, 256)


def count_hops(place, far):
    return [across(place, d) for d in ("y", "l", "h")] + far_hops(place, far)


def layer_kernel(far, names, *refs):
    r = SimpleNamespace(**dict(zip(names, refs)))
    extra = refs[len(names) :]
    r.boxes, r.core_boxes = extra[: len(extra) - 10], extra[len(extra) - 10 :]
    place = coordinates()
    x, core = place["x"], place["core"]
    half, width = r.row_tokens.shape
    cols = half // 2
    ff = r.hidden.shape[1]
    tile = 256
    chunks = chunks_of(far)
    n = len(chunks)
    boxes = [r.boxes[i] for i in range(n)]
    core_boxes = [r.core_boxes[i] for i in range(9)]
    core_boxes += [
        r.down_weight.at[pl.ds(3 * width, width), pl.ds(i * 384, 384)] for i in range(2)
    ]
    core_boxes.append(r.core_boxes[9])
    own = dict(down=r.down_own, up=r.up_own, out=r.up_weight.at[:, pl.ds(3 * width, width)], into=r.up_weight)
    whole = dict(down=r.down_whole, up=r.up_whole, out=r.out_whole, into=r.into_whole)
    other_x = device_at(place, x=1 - x)
    other_core = device_at(place, core=1 - core)
    here, there = here_of(x, cols), here_of(1 - x, cols)
    row_tokens, row_cot = r.row_tokens, r.row_cot
    query, keys, values, bias = r.query, r.keys, r.values, r.bias
    attended, log_total = r.attended, r.log_total
    in_first, in_later = r.down_own, r.down_weight
    out_weight, up_weight, down_weight = r.out_weight, r.up_weight, r.down_weight

    def local(source, target, sem):
        copy = pltpu.make_async_copy(source, target, sem)
        copy.start()
        return copy

    def load_in(target, sems):
        return [
            local(
                r.into_any.at[:, pl.ds(j * width, width)],
                target.at[pl.ds(j * width, width), :],
                sems.at[j],
            )
            for j in range(3)
        ]

    stay_tokens = local(r.tokens_any.at[x], row_tokens.at[here], r.stay_sems.at[0])
    in_loads = load_in(in_first, r.in_sems)
    stay_cot = local(r.cot_any.at[x], row_cot.at[here], r.stay_sems.at[1])
    weight_loads = [
        local(a, b, r.load_sems.at[i])
        for i, (a, b) in enumerate(
            (
                (r.out_any, r.out_weight),
                (r.up_any, r.up_weight),
                (r.down_any, r.down_weight),
            )
        )
    ]
    greet(place, far)
    row_send, row_recv = r.row_send, r.row_recv
    move_tokens = remote(
        r.tokens_any.at[1 - x], row_tokens.at[here], row_send.at[0], row_recv.at[0], other_x
    )
    move_tokens.start()
    ids_out, ids_in = r.ids_out, r.ids_in
    for i in range(2):
        ids_out[i] = jnp.broadcast_to(r.segments[i : i + 1, :], (8, cols))
    blk = x * 2 + core
    moves = []
    for i, (dx, dc) in enumerate(((0, 1), (1, 0), (1, 1))):
        to_x = x + dx - 2 * dx * x
        to_core = core + dc - 2 * dc * core
        moves.append(
            remote(
                ids_out.at[to_x],
                ids_in.at[blk],
                r.id_send.at[i],
                r.id_recv.at[i],
                device_at(place, x=to_x, core=to_core),
            )
        )
        moves[-1].start()
    ids_in[blk] = ids_out[x]
    counts, count_in, keep = r.counts, r.count_in, r.keep
    counts[0] = jnp.full((8, 128), (keep[0] + keep[1]).astype(F32), F32)
    hops = count_hops(place, far)
    count_moves = []

    def hop(i):
        if i:
            count_moves[-1].wait_recv()
            counts[i] = counts[i - 1] + count_in[i - 1]
        if i < len(hops):
            move = remote(
                counts.at[i], count_in.at[i], r.count_send.at[i], r.count_recv.at[i], hops[i]
            )
            move.start()
            count_moves.append(move)

    hop(0)
    move_cot = remote(
        r.cot_any.at[1 - x], row_cot.at[here], row_send.at[1], row_recv.at[1], other_x
    )

    def as_row(ref, part=slice(None)):
        return ref[part].astype(F32).reshape(1, -1)

    def project(rows, at):
        block = row_tokens[rows, :]
        place_rows = span(core * half + at, cols, 256)
        keys[place_rows, :] = dot(block, in_first[width : 2 * width, :]).astype(LOW)
        values[place_rows, :] = (
            dot(block, in_first[2 * width : 3 * width, :]) + as_row(r.value_bias)
        ).astype(LOW)
        return place_rows

    def project_query(rows):
        block = row_tokens[rows, :]
        query[rows, :] = (dot(block, in_first[:width, :]) + as_row(r.query_bias)).astype(
            LOW
        ) * jnp.asarray(HEAD_DIM**-0.5, LOW)

    shares = []
    stay_tokens.wait()
    for load in in_loads:
        load.wait()
    for step, (rows, at) in enumerate(((here, x * cols), (there, (1 - x) * cols))):
        if step == 1:
            move_tokens.wait_recv()
            move_cot.start()
        place_rows = project(rows, at)
        for i, array in enumerate((keys, values)):
            k = step * 2 + i
            move = remote(
                array.at[place_rows],
                array.at[place_rows],
                r.share_send.at[k],
                r.share_recv.at[k],
                other_core,
            )
            move.start()
            shares.append(move)
        project_query(rows)
        hop(1 + step)
    for move in moves:
        move.wait_recv()
    all_ids = jnp.concatenate([ids_in[0], ids_in[2], ids_in[1], ids_in[3]], axis=1).astype(F32)
    column = jnp.broadcast_to(all_ids[0:1, :], (128, 2 * half)).T[:, 0:1]
    own_ids = jnp.concatenate([ids_in[core], ids_in[2 + core]], axis=1).astype(F32)[0:1, :]
    bias[...] = jnp.where(column == own_ids, 0.0, masked_score).astype(LOW)
    for i in range(3, len(hops) + 1):
        hop(i)
    factor = keep[x].astype(F32) * (float(2 * 8 * far) / counts[len(hops)])[0:1, 0:1]
    r.kept[...] = counts[len(hops)].astype(jnp.int32)
    for move in shares:
        move.wait_recv()

    def attend(p, carry):
        pair = span(p * PAIR, PAIR, PAIR)
        values_t = values[:, pair].T
        key_pair = keys[:, pair]
        query_pair = query[:, pair]
        scores = []
        for i in range(2):
            chosen = jnp.where(lanes_of(i, half), query_pair, jnp.zeros_like(query_pair))
            scores.append(dot_nt(key_pair, chosen) + bias[...].astype(F32))
        for i in range(2):
            top = jnp.max(scores[i], axis=0, keepdims=True)
            powered = jnp.exp(scores[i] - top)
            total = jnp.sum(powered, axis=0, keepdims=True)
            mixture = dot(values_t[i * HEAD_DIM : (i + 1) * HEAD_DIM, :], powered.astype(LOW))
            attended[span(p * PAIR + i * HEAD_DIM, HEAD_DIM, HEAD_DIM), :] = mixture / total
            log_total[pl.ds(p * 2 + i, 1), :] = top + jnp.log(total)
        return carry

    lax.fori_loop(0, width // PAIR, attend, 0)

    low, work, normed = r.low, r.work, r.normed
    inverse, first, first_low, first_t = r.inverse, r.first, r.first_low, r.first_t
    hidden, slope, vectors = r.hidden, r.slope, r.vec_totals.at[0]
    second_in, ffn_grad, attended_grad = first, first_low, low
    low[...] = attended[...].T.astype(LOW)
    weight_loads[0].wait()
    work[...] = dot(low[...], out_weight[...])
    mean = partial(jnp.mean, axis=-1, keepdims=True)

    def tiles(step, carry):
        def one(t, kept):
            return step(span(t * tile, tile, tile), kept)

        return lax.fori_loop(0, half // tile, one, carry)

    def normalize(given):
        centered = given - mean(given)
        inv = lax.rsqrt(mean(centered * centered) + norm_eps)
        return centered * inv, inv

    def total_of(given):
        return jnp.sum(given, axis=0, keepdims=True)

    def first_norm(at, carry):
        branch = work[at, :] + as_row(r.out_bias)
        unit, inv = normalize(row_tokens[at, :].astype(F32) + factor * branch)
        normed[at, :] = unit
        inverse[at, :] = jnp.broadcast_to(inv, (tile, 128))
        out = unit * as_row(r.first_gain) + as_row(r.first_shift)
        first[at, :] = out
        first_low[at, :] = out.astype(LOW)
        return carry

    tiles(first_norm, 0)
    first_t[...] = first_low[...].T
    weight_loads[1].wait()

    def up_step(f, carry):
        at = span(f * 512, 512, 512)
        pre = dot(first_low[...], up_weight[:, at]) + as_row(r.up_bias, at)
        chance = 0.5 + 0.5 * lax.erf(pre * (2.0**-0.5))
        density = jnp.exp(pre * pre * -0.5) * 0.3989422804014327
        hidden[:, at] = (pre * chance).astype(LOW)
        slope[:, at] = (chance + pre * density).astype(LOW)
        return carry

    lax.fori_loop(0, ff // 512, up_step, 0)
    weight_loads[2].wait()
    work[...] = dot(hidden[...], down_weight[...])
    zero = jnp.zeros((1, width), F32)
    move_cot.wait_recv()
    stay_cot.wait()

    def second_norm(at, carry):
        gain_sum, shift_sum, bias_sum = carry
        gain = as_row(r.second_gain)
        unit, inv = normalize(first[at, :] + factor * (work[at, :] + as_row(r.down_bias)))
        grad = row_cot[at, :].astype(F32)
        row_cot[at, :] = (unit * gain + as_row(r.second_shift)).astype(LOW)
        scaled = grad * gain
        inner = inv * (scaled - mean(scaled) - unit * mean(scaled * unit))
        second_in[at, :] = inner
        low_grad = (factor * inner).astype(LOW)
        ffn_grad[at, :] = low_grad
        return (
            gain_sum + total_of(grad * unit),
            shift_sum + total_of(grad),
            bias_sum + total_of(low_grad.astype(F32)),
        )

    second_gain_sum, second_shift_sum, down_sum = tiles(second_norm, (zero, zero, zero))
    vectors[...] = jnp.zeros_like(vectors)
    vectors[5:6, :] = down_sum
    vectors[6:7, :] = second_gain_sum
    vectors[7:8, :] = second_shift_sum
    mixed, tokens_grad = r.mixed, r.tokens_grad
    move_mixed = remote(row_cot.at[there], mixed.at[x], row_send.at[2], row_recv.at[2], other_x)
    move_mixed.start()
    stay_mixed = local(row_cot.at[here], mixed.at[x], r.stay_sems.at[2])

    offsets = [sum(c.copies for c in chunks[:i]) for i in range(n)]
    gens = {}

    def advance(i):
        if i == n and i not in gens:
            gens[i] = vector_steps(place, far, r.vec_totals, r.vec_inbox, r.vec_send, r.vec_recv)
        if i not in gens:
            part = pl.ds(offsets[i], chunks[i].copies)
            gens[i] = chunks[i].steps(
                place,
                own[chunks[i].matrix],
                whole[chunks[i].matrix],
                core_boxes[i],
                boxes[i],
                r.send_sems.at[part],
                r.recv_sems.at[part],
                r.store_sems.at[i],
            )
        next(gens[i], None)

    def down_part(f):
        at = pl.ds(f * width, width)
        own["down"][at, :] = dot(hidden[:, at].T, ffn_grad[...]).astype(LOW)

    def feed_back(f):
        at = pl.ds(f * width, width)
        pulled = dot_nt(ffn_grad[...], down_weight[at, :])
        pre_grad = (slope[:, at].astype(F32) * pulled).astype(LOW)
        own["up"][:, at] = dot(first_t[...], pre_grad).astype(LOW)
        part = dot_nt(pre_grad, up_weight[:, at])
        if f:
            work[...] += part
        else:
            work[...] = part
        vectors[8 + f : 9 + f, :] = total_of(pre_grad.astype(F32))

    tokens_t, delta = first_t, r.delta
    in_again = []

    def first_back(at, carry):
        gain_sum, shift_sum, bias_sum = carry
        grad = second_in[at, :] + work[at, :]
        unit = normed[at, :]
        scaled = grad * as_row(r.first_gain)
        inner = inverse[at, 0:1] * (scaled - mean(scaled) - unit * mean(scaled * unit))
        work[at, :] = inner
        low_grad = (factor * inner).astype(LOW)
        ffn_grad[at, :] = low_grad
        return (
            gain_sum + total_of(grad * unit),
            shift_sum + total_of(grad),
            bias_sum + total_of(low_grad.astype(F32)),
        )

    def norm_back():
        in_again.extend(load_in(in_later, r.in_sems))
        first_gain_sum, first_shift_sum, out_sum = tiles(first_back, (zero, zero, zero))
        vectors[2:3, :] = out_sum
        vectors[3:4, :] = first_gain_sum
        vectors[4:5, :] = first_shift_sum
        branch_grad = ffn_grad[...]
        own["out"][...] = dot(attended[...].astype(LOW), branch_grad).astype(LOW)
        attended_grad[...] = dot_nt(branch_grad, out_weight[...]).astype(LOW)
        product = dot_nt(out_weight[...], branch_grad).astype(LOW).astype(F32) * attended[...]
        delta[...] = jnp.zeros_like(delta)
        for h in range(width // HEAD_DIM):
            delta[h : h + 1, :] = total_of(product[h * HEAD_DIM : (h + 1) * HEAD_DIM, :])
        tokens_t[...] = row_tokens[...].T

    query_t, joined, other, arrived = attended, hidden, slope, r.arrived
    mine = (normed, first)
    pair_moves = []

    def one_side(p, side, fresh):
        pair = pl.ds(p * PAIR, PAIR)
        at = span(side * half, half, 512)
        key_pair, value_pair = keys[at, pair], values[at, pair]
        keys_t = key_pair.T
        query_pair, grad_pair = query[:, pair], attended_grad[:, pair]
        none = jnp.zeros_like(query_pair)
        heads = [pl.ds(p * 2 + i, 1) for i in range(2)]
        chosen = [jnp.where(lanes_of(i, half), query_pair, none) for i in range(2)]
        pulled = [jnp.where(lanes_of(i, half), grad_pair, none) for i in range(2)]
        mask = bias[at, :].astype(F32)
        scores = [dot_nt(key_pair, chosen[i]) + mask for i in range(2)]
        pull = [dot_nt(value_pair, pulled[i]) - delta[heads[i], :] for i in range(2)]
        chance = [jnp.exp(scores[i] - log_total[heads[i], :]) for i in range(2)]
        score_grad = [(chance[i] * pull[i]).astype(LOW) for i in range(2)]
        value_sum = sum(dot(chance[i].astype(LOW), pulled[i]) for i in range(2))
        key_sum = sum(dot(score_grad[i], chosen[i]) for i in range(2))
        for i in range(2):
            lines = pl.ds(p * PAIR + i * HEAD_DIM, HEAD_DIM)
            query_part = dot(keys_t[i * HEAD_DIM : (i + 1) * HEAD_DIM, :], score_grad[i])
            if fresh:
                query_t[lines, :] = query_part
            else:
                query_t[lines, :] += query_part
        return key_sum, value_sum

    def attend_back(p, mine_too):
        pair = pl.ds(p * PAIR, PAIR)
        if mine_too:
            key_sum, value_sum = one_side(p, core, False)
            mine[0][:, pair] = key_sum
            mine[1][:, pair] = value_sum
            return
        for i, part in enumerate(one_side(p, 1 - core, True)):
            at = pl.ds(i * width + p * PAIR, PAIR)
            other[:, at] = part.astype(LOW)
            k = p * 2 + i
            move = remote(
                other.at[:, at],
                arrived.at[:, at],
                r.pair_send.at[k],
                r.pair_recv.at[k],
                other_core,
            )
            move.start()
            pair_moves.append(move)

    def join(j, at):
        to = pl.ds(j * width + at.start, at.size)
        if j == 0:
            joined[:, to] = (query_t[at, :].T * HEAD_DIM**-0.5).astype(LOW)
        else:
            sent = pl.ds((j - 1) * width + at.start, at.size)
            joined[:, to] = (mine[j - 1][:, at] + arrived[:, sent].astype(F32)).astype(LOW)
        own["into"][:, to] = dot(tokens_t[...], joined[:, to]).astype(LOW)

    def wait_pairs(start, stop):
        for move in pair_moves[2 * start : 2 * stop]:
            move.wait_recv()

    some, rest, every = pl.ds(0, width // 2), pl.ds(width // 2, width // 2), pl.ds(0, width)
    pairs = width // PAIR

    def join_some():
        wait_pairs(0, pairs // 2)
        join(0, some)
        join(1, some)

    def join_values():
        wait_pairs(pairs // 2, pairs)
        join(2, every)

    def join_rest():
        join(0, rest)
        join(1, rest)
        for i, j in ((0, 0), (1, 2)):
            vectors[i : i + 1, :] = total_of(joined[:, j * width : (j + 1) * width].astype(F32))

    row_grad = slope.at[:, pl.ds(2 * width, width)]
    last_moves = []

    def finish_rows():
        for load in in_again:
            load.wait()
        total = work[...]
        for j in range(3):
            at = pl.ds(j * width, width)
            total = total + dot_nt(joined[:, at], in_later[at, :])
        row_grad[...] = total.astype(LOW)
        last_moves.append(
            remote(row_grad.at[there], tokens_grad.at[x], row_send.at[3], row_recv.at[3], other_x)
        )
        last_moves[0].start()
        last_moves.append(local(row_grad.at[here], tokens_grad.at[x], r.stay_sems.at[3]))

    halves = [partial(attend_back, p, side) for p in range(pairs) for side in (False, True)]
    pieces = [partial(down_part, f) for f in range(ff // width)]
    pieces += [partial(feed_back, f) for f in range(ff // width)] + [norm_back]
    pieces += [*halves[:8], join_some, *halves[8:], join_values, join_rest, finish_rows]
    for turn in PLAN:
        if turn <= n:
            advance(turn)
        else:
            pieces[turn - n - 1]()
    for i in range(n + 1):
        for _ in gens[i]:
            pass
    r.vector_out[...] = r.vec_totals[len(vector_hops(place, far))]
    stay_mixed.wait()
    move_mixed.wait()
    for move in last_moves:
        move.wait()
    for move in [move_tokens, move_cot, *moves, *count_moves, *shares, *pair_moves]:
        move.wait_send()


def layer(tokens, cot, segments, keep, weights, vectors, far):
    _, cols, width = tokens.shape
    half = 2 * cols
    ff = weights[2].shape[1]
    chunks = chunks_of(far)
    hops = 5 + len(far_bits(far))
    counts = 3 + len(far_bits(far))
    copies = sum(c.copies for c in chunks)
    vmem, any_space = pl.BlockSpec(memory_space=pltpu.VMEM), pl.BlockSpec(memory_space=pl.ANY)
    smem = pl.BlockSpec(memory_space=pltpu.SMEM)
    shape = jax.ShapeDtypeStruct

    def dma(count):
        return pltpu.SemaphoreType.DMA((count,))

    inputs = dict(
        tokens_any=(tokens, any_space),
        cot_any=(cot, any_space),
        segments=(segments, vmem),
        keep=(keep, smem),
        into_any=(weights[0], any_space),
        out_any=(weights[1], any_space),
        up_any=(weights[2], any_space),
        down_any=(weights[3], any_space),
        **{k: (v, vmem) for k, v in vectors.items()},
    )
    outputs = dict(
        into_whole=(shape((width, 3 * width), LOW), any_space),
        out_whole=(shape((width, width), LOW), any_space),
        up_whole=(shape((width, ff), LOW), any_space),
        down_whole=(shape((ff, width), LOW), any_space),
        vector_out=(shape((16, width), F32), vmem),
        mixed=(shape(tokens.shape, LOW), any_space),
        tokens_grad=(shape(tokens.shape, LOW), any_space),
        kept=(shape((8, 128), jnp.int32), vmem),
    )
    scratch = dict(
        out_weight=((width, width), LOW),
        up_weight=((width, ff), LOW),
        down_weight=((ff, width), LOW),
        up_own=((width, ff), LOW),
        down_own=((ff, width), LOW),
        row_tokens=((half, width), LOW),
        row_cot=((half, width), LOW),
        query=((half, width), LOW),
        keys=((2 * half, width), LOW),
        values=((2 * half, width), LOW),
        bias=((2 * half, half), LOW),
        attended=((width, half), F32),
        log_total=((16, half), F32),
        delta=((16, half), F32),
        low=((half, width), LOW),
        work=((half, width), F32),
        normed=((half, width), F32),
        inverse=((half, 128), F32),
        first=((half, width), F32),
        first_low=((half, width), LOW),
        first_t=((width, half), LOW),
        hidden=((half, ff), LOW),
        slope=((half, ff), LOW),
        arrived=((half, 2 * width), LOW),
        ids_out=((2, 8, cols), jnp.int32),
        ids_in=((4, 8, cols), jnp.int32),
        counts=((counts + 1, 8, 128), F32),
        count_in=((counts, 8, 128), F32),
        vec_inbox=((hops, 16, width), F32),
        vec_totals=((hops + 1, 16, width), F32),
    )
    sems = dict(
        in_sems=3,
        load_sems=3,
        stay_sems=4,
        row_send=4,
        row_recv=4,
        id_send=3,
        id_recv=3,
        count_send=counts,
        count_recv=counts,
        share_send=4,
        share_recv=4,
        pair_send=2 * width // PAIR,
        pair_recv=2 * width // PAIR,
        send_sems=copies,
        recv_sems=copies,
        store_sems=len(chunks),
        vec_send=hops,
        vec_recv=hops,
    )
    boxes = [((c.received, c.width), LOW) for c in chunks]
    boxes += [((width, c.width), LOW) for c in chunks[:10]]
    names = [*inputs, *outputs, *scratch, *sems]
    return pl.pallas_call(
        partial(layer_kernel, far, names),
        out_shape=[o[0] for o in outputs.values()],
        in_specs=[i[1] for i in inputs.values()],
        out_specs=[o[1] for o in outputs.values()],
        scratch_shapes=[pltpu.VMEM(a, t) for a, t in scratch.values()]
        + [dma(c) for c in sems.values()]
        + [pltpu.VMEM(a, t) for a, t in boxes],
        compiler_params=pltpu.CompilerParams(
            collective_id=0, has_side_effects=True, vmem_limit_bytes=VMEM_LIMIT
        ),
        name="layer",
    )(*[i[0] for i in inputs.values()])


def finish_kernel(*refs):
    given, (vectors, kept, mixed, tokens_grad), outs = refs[:4], refs[4:8], refs[8:12]
    (query_b, value_b, out_b, first_g, first_s, up_b, down_b, second_g, second_s) = refs[12:21]
    kept_out, mixed_out, tokens_out = refs[21:24]
    low, wide, load_sems, store_sems, row_sems = refs[24:28], refs[28:32], *refs[32:35]
    held = refs[35:37]
    rows_in = [
        pltpu.make_async_copy(a, b, row_sems.at[i])
        for i, (a, b) in enumerate(zip((mixed, tokens_grad), held))
    ]
    rows_out = [
        pltpu.make_async_copy(a, b, row_sems.at[2 + i])
        for i, (a, b) in enumerate(zip(held, (mixed_out, tokens_out)))
    ]
    tiles = []
    for m, ref in enumerate(given):
        height = 196608 // ref.shape[1] // 16 * 16
        height = next(h for h in range(height, 0, -16) if ref.shape[0] % h == 0)
        tiles += [(m, pl.ds(at, height)) for at in range(0, ref.shape[0], height)]
    loads = [
        pltpu.make_async_copy(given[m].at[at], low[m].at[at], load_sems.at[i])
        for i, (m, at) in enumerate(tiles)
    ]
    stores = [
        pltpu.make_async_copy(wide[m].at[at], outs[m].at[at], store_sems.at[i])
        for i, (m, at) in enumerate(tiles)
    ]
    for load in loads:
        load.start()
    for row in rows_in:
        row.start()
    small = (query_b, value_b, out_b, first_g, first_s, down_b, second_g, second_s)
    kept_out[...] = kept[0:1, 0:1].reshape((1,))
    for i, ref in enumerate(small):
        ref[...] = vectors[i : i + 1, :].reshape(ref.shape)
    width = vectors.shape[1]
    for i in range(up_b.shape[0] // width):
        up_b[pl.ds(i * width, width)] = vectors[8 + i : 9 + i, :].reshape((width,))
    for load, store, (m, at) in zip(loads, stores, tiles):
        load.wait()
        piece = 32 if at.size % 32 == 0 else 16

        def convert(t, carry):
            part = span(at.start + t * piece, piece, 16)
            wide[m][part, :] = low[m][part, :].astype(F32)
            return carry

        lax.fori_loop(0, at.size // piece, convert, 0)
        store.start()
    for row_in, row_out in zip(rows_in, rows_out):
        row_in.wait()
        row_out.start()
    for copy in [*stores, *rows_out]:
        copy.wait()


def finish(matrices, vectors, kept, mixed, tokens_grad):
    width = vectors.shape[1]
    ff = matrices[2].shape[1]
    vmem, any_space = pl.BlockSpec(memory_space=pltpu.VMEM), pl.BlockSpec(memory_space=pl.ANY)
    shape = jax.ShapeDtypeStruct
    sizes = [width, width, width, width, width, ff, width, width, width]
    return pl.pallas_call(
        finish_kernel,
        out_shape=[shape(m.shape, F32) for m in matrices]
        + [shape((k,), F32) for k in sizes]
        + [shape((1,), jnp.int32), shape(mixed.shape, LOW), shape(tokens_grad.shape, LOW)],
        in_specs=[any_space] * 4 + [vmem] * 2 + [any_space] * 2,
        out_specs=[any_space] * 4 + [vmem] * 10 + [any_space] * 2,
        scratch_shapes=[pltpu.VMEM(m.shape, LOW) for m in matrices]
        + [pltpu.VMEM(m.shape, F32) for m in matrices]
        + [
            pltpu.SemaphoreType.DMA((64,)),
            pltpu.SemaphoreType.DMA((64,)),
            pltpu.SemaphoreType.DMA((4,)),
            pltpu.VMEM(mixed.shape, LOW),
            pltpu.VMEM(tokens_grad.shape, LOW),
        ],
        compiler_params=pltpu.CompilerParams(vmem_limit_bytes=VMEM_LIMIT),
        name="finish",
    )(*matrices, vectors, kept, mixed, tokens_grad)


def body(
    tokens,
    segment_ids,
    keep_flags,
    input_weight,
    query_bias,
    value_bias,
    output_weight,
    output_bias,
    first_gain,
    first_shift,
    up_weight,
    up_bias,
    down_weight,
    down_bias,
    second_gain,
    second_shift,
    cotangent,
):
    far = lax.axis_size("batch") // 8
    *low, vectors, mixed, tokens_grad, kept = layer(
        tokens,
        cotangent,
        segment_ids,
        keep_flags,
        (input_weight, output_weight, up_weight, down_weight),
        dict(
            query_bias=query_bias,
            value_bias=value_bias,
            out_bias=output_bias,
            first_gain=first_gain,
            first_shift=first_shift,
            up_bias=up_bias,
            down_bias=down_bias,
            second_gain=second_gain,
            second_shift=second_shift,
        ),
        far,
    )
    into, out, up, down, *small, kept, mixed, tokens_grad = finish(
        low, vectors, kept, mixed, tokens_grad
    )
    query_b, value_b, out_b, first_g, first_s, up_b, down_b, second_g, second_s = small
    return (
        mixed,
        tokens_grad,
        kept.reshape(()),
        into,
        query_b,
        value_b,
        out,
        out_b,
        first_g,
        first_s,
        up,
        up_b,
        down,
        down_b,
        second_g,
        second_s,
    )


def solution(mesh):
    in_specs = (
        P("batch", "blk", None),
        P("batch", "blk"),
        P("batch"),
        P(),
        P(),
        P(),
        P(),
        P(),
        P(),
        P(),
        P(),
        P(),
        P(),
        P(),
        P(),
        P(),
        P("batch", "blk", None),
    )
    out_specs = (
        P("batch", "blk", None),
        P("batch", "blk", None),
        P(),
        P(),
        P(),
        P(),
        P(),
        P(),
        P(),
        P(),
        P(),
        P(),
        P(),
        P(),
        P(),
        P(),
    )
    return jax.shard_map(body, mesh=mesh, in_specs=in_specs, out_specs=out_specs, check_vma=False)
```
